256 devices in a mesh: tgt: 64 (over z, y, core), src: 4 (over x).
Axes of the slice: x: 4, y: 4, z: 8, core: 2. Of those that a mesh axis runs over, the one named last changes fastest.
Arguments:
- tgt_coords: bfloat16 [3, 262144], P(None, 'tgt'), may hold values from -1 to 1
- tgt_embed: bfloat16 [64, 262144], P(None, 'tgt'), may hold values from -3 to 3
- tile_perm: int32 [512], P('tgt'), may hold values from 0 to 511, each once
- tile_count: int32 [512], replicated, may hold values from 1 to 512, as said below
- src_coords: bfloat16 [3, 32768], P(None, ('tgt', 'src')), may hold values from -1 to 1
- src_embed: bfloat16 [64, 32768], P(None, ('tgt', 'src')), may hold values from -3 to 3
- anchors: float32 [3, 256], replicated, may hold values from -1 to 1
- sigma2: float32 [1], replicated, may hold values from 0.2 to 1
- outlier_weight: float32 [1], replicated, may hold values from 0.1 to 0.5
- warp_lambda: float32 [1], replicated, may hold values from 0.05 to 0.5
Outputs:
- warped: float32 [3, 32768], P(None, ('tgt', 'src'))
- masses: float32 [32768], P(('tgt', 'src'))
The draws below stay inside these ranges and needn't reach their ends.
Inputs may be any that keep to these rules, and one draw needn't show every extreme that they name: `tile_count`: one spatial tile has all 512 cells valid.
All inputs are finite; a program needn't handle non-finite values.
Results may differ from the reference program's by a relative error of at most 0.0003.
Values may be sent and summed in bfloat16 or wider, within the bound.
No kernel may reach another device: no remote copies, remote signals or barrier semaphores. Data moves between devices by JAX's collectives and lax.ppermute only.
A program may use at most 64 MiB of HBM per device.

```python
import math
import jax
import jax.numpy as jnp
from jax import lax

E = 64
ANCHORS = 256
TILE = 512
PIECE = 128
TGT_DEV = 4096
TILES = 512
N = 262144
M = 32768
N_TGT = 64
N_SRC = 4


CLUSTERS = 5


def draw_tile_count(key, part):
    key = jax.random.fold_in(key, 7)
    key_count, key_spot = jax.random.split(key)
    counts = jax.random.randint(key_count, (TILES,), 1, TILE + 1, dtype=jnp.int32)
    spot = jax.random.randint(key_spot, (), 0, TILES, dtype=jnp.int32)
    return counts.at[spot].set(TILE)


def draw_src_coords(key, part):
    key = jax.random.fold_in(key, 11)
    key_pick, key_centre, key_along, key_rest = jax.random.split(key, 4)
    cells = jnp.arange(M, dtype=jnp.int32)
    band = (cells // PIECE % N_SRC).astype(jnp.float32)
    pick = jax.random.randint(key_pick, (M,), 0, CLUSTERS, dtype=jnp.int32)
    centres = jax.random.uniform(key_centre, (2, CLUSTERS), jnp.float32, -0.7, 0.7)
    centre = centres[:, pick]
    along = jnp.clip(0.5 + 0.12 * jax.random.normal(key_along, (M,), jnp.float32), 0.0, 1.0)
    offset = 0.1 * jax.random.normal(key_rest, (2, M), jnp.float32)
    first = -1.0 + (band + along) * (2.0 / N_SRC)
    rest = jnp.clip(centre + offset, -1.0, 1.0)
    return jnp.concatenate([first[None, :], rest], axis=0).astype(jnp.bfloat16)


def levels(stream_key, dims, pieces, low, high):
    loudness, own = 1.0, jax.random.fold_in(stream_key, 6)
    for position, parts in pieces:
        draws = jnp.exp(jax.random.uniform(jax.random.fold_in(own, position), (parts,), jnp.float32, low / len(pieces), high / len(pieces)))
        loudness = loudness * jnp.repeat(draws, dims[position] // parts).reshape([-1 if axis == position else 1 for axis in range(len(dims))])
    return loudness


def gaussian(rng, dims, width, limit, pieces=(), kind=jnp.bfloat16):
    loudness = levels(rng, dims, pieces, -0.22, 0.18) if pieces else 1.0
    entries = jax.random.normal(rng, dims, jnp.float32) * width * loudness
    return jnp.minimum(jnp.maximum(entries, -limit), limit).astype(kind)


def setup_inputs(seed: int = 0) -> dict:
    key_of = jax.random.split(jax.random.key(seed), 11)
    return {
        "tgt_coords": jnp.clip(jax.random.uniform(key_of[0], (3, N), jnp.float32, -1.0, 1.0) * levels(key_of[0], (3, N), ((1, 64),), -0.4, 0.0), -1.0, 1.0).astype(jnp.bfloat16),
        "tgt_embed": gaussian(key_of[1], (E, N), 1.0, 3.0, ((1, 64),)),
        "tile_perm": jax.random.permutation(key_of[2], TILES).astype(jnp.int32),
        "tile_count": draw_tile_count(jax.random.fold_in(key_of[10], 71), 0),
        "src_coords": draw_src_coords(jax.random.fold_in(key_of[10], 71), 0),
        "src_embed": gaussian(key_of[5], (E, M), 1.0, 3.0, ((1, 256),)),
        "anchors": jnp.clip(jax.random.uniform(key_of[6], (3, ANCHORS), jnp.float32, -1.0, 1.0), -1.0, 1.0),
        "sigma2": jnp.clip(jnp.exp(jax.random.uniform(key_of[7], (1,), jnp.float32, math.log(0.2), math.log(1.0))), 0.2, 1.0),
        "outlier_weight": jnp.clip(jax.random.uniform(key_of[8], (1,), jnp.float32, 0.1, 0.5), 0.1, 0.5),
        "warp_lambda": jnp.clip(jnp.exp(jax.random.uniform(key_of[9], (1,), jnp.float32, math.log(0.05), math.log(0.5))), 0.05, 0.5),
    }


SCORE_GAIN = 4.0
ANCHOR_WIDTH = 0.1

def cell_mask(tile_perm, tile_count):
    tiles_all = tile_count.shape[0]
    hits = tile_perm[:, None] == jnp.arange(tiles_all, dtype=jnp.int32)[None, :]
    counts = jnp.sum(jnp.where(hits, tile_count[None, :], 0), axis=1)
    within = jnp.arange(TILE, dtype=jnp.int32)
    return (within[None, :] < counts[:, None]).astype(jnp.float32).reshape(-1)

def squared_gap(first, second):
    gap_a = first[0][:, None] - second[0][None, :]
    gap_b = first[1][:, None] - second[1][None, :]
    gap_c = first[2][:, None] - second[2][None, :]
    return gap_a * gap_a + gap_b * gap_b + gap_c * gap_c

def affinity(src_xyz, src_feat, tgt_xyz, tgt_feat, keep, inv_spread):
    similar = lax.dot_general(src_feat.astype(jnp.float32), tgt_feat.astype(jnp.float32), (((0,), (0,)), ((), ())), preferred_element_type=jnp.float32)
    scale = SCORE_GAIN / src_feat.shape[0]
    return jnp.exp(similar * scale - squared_gap(src_xyz, tgt_xyz) * inv_spread) * keep[None, :]

def moments(posterior, tgt_xyz):
    weights = jnp.concatenate([jnp.ones_like(tgt_xyz[:1]), tgt_xyz], axis=0)
    return lax.dot_general(weights.astype(jnp.float32), posterior.astype(jnp.float32), (((1,), (1,)), ((), ())), precision=lax.Precision.HIGHEST, preferred_element_type=jnp.float32)

def warp_terms(src_xyz, anchors, masses, moved):
    basis = jnp.exp(-squared_gap(src_xyz, anchors) * (0.5 / ANCHOR_WIDTH))
    gram = lax.dot_general(basis.astype(jnp.float32), (masses[:, None] * basis).astype(jnp.float32), (((0,), (0,)), ((), ())), precision=lax.Precision.HIGHEST, preferred_element_type=jnp.float32)
    pulled = jnp.dot(moved - masses[None, :] * src_xyz, basis, precision=lax.Precision.HIGHEST)
    return (basis, gram, pulled, jnp.sum(masses))

def warp_solve(basis, gram, pulled, total, anchors, sigma2, warp_lambda):
    anchor_gram = jnp.exp(-squared_gap(anchors, anchors) * (0.5 / ANCHOR_WIDTH))
    system = gram / total + warp_lambda[0] * sigma2[0] * (anchor_gram + jnp.eye(anchors.shape[1], dtype=jnp.float32))
    factor = jnp.linalg.cholesky(system)
    coeffs = jax.scipy.linalg.cho_solve((factor, True), (pulled / total).T)
    return lax.dot_general(coeffs.astype(jnp.float32), basis.astype(jnp.float32), (((0,), (1,)), ((), ())), precision=lax.Precision.HIGHEST, preferred_element_type=jnp.float32)

def reference(tgt_coords, tgt_embed, tile_perm, tile_count, src_coords, src_embed, anchors, sigma2, outlier_weight, warp_lambda):
    keep_all = cell_mask(tile_perm, tile_count)
    src_xyz = src_coords.astype(jnp.float32)
    inv_spread = 0.5 / sigma2[0]
    floor_term = outlier_weight[0] / (1.0 - outlier_weight[0]) * src_coords.shape[1]
    tgt_xyz = tgt_coords.astype(jnp.float32).reshape(3, N_TGT, TGT_DEV).transpose(1, 0, 2)
    tgt_feat = tgt_embed.reshape(E, N_TGT, TGT_DEV).transpose(1, 0, 2)
    keeps = keep_all.reshape(N_TGT, TGT_DEV)

    def visit(carry, item):
        xyz, feat, keep = item
        kernel = affinity(src_xyz, src_embed, xyz, feat, keep, inv_spread)
        normal = jnp.sum(kernel, axis=0) + floor_term
        return (carry + moments(kernel / normal[None, :], xyz), None)
    sums, unused = lax.scan(visit, jnp.zeros((4, src_coords.shape[1]), jnp.float32), (tgt_xyz, tgt_feat, keeps))
    masses = sums[0]
    basis, gram, pulled, total = warp_terms(src_xyz, anchors, masses, sums[1:])
    shift = warp_solve(basis, gram, pulled, total, anchors, sigma2, warp_lambda)
    return (src_xyz + shift, masses)
```

```python
import functools
import math

import jax
import jax.numpy as jnp
from jax import lax
from jax.experimental import pallas as pl
from jax.experimental.pallas import tpu as pltpu
from jax.sharding import Mesh
from jax.sharding import PartitionSpec as P

TILE = 512
SCORE_GAIN = 4.0
ANCHOR_WIDTH = 0.1
LOG2E = math.log2(math.e)

ROWS = 256
LANES = 128
DEPTH = 256
STORED = 14
MASKED = -30000.0
HALF = 232
WARP_ROWS = 200

F32 = jnp.float32
BF16 = jnp.bfloat16
WHOLE = pl.BlockSpec(memory_space=pltpu.VMEM)
SCALAR = pl.BlockSpec(memory_space=pltpu.SMEM)


def split3(value):
    high = value.astype(BF16).astype(F32)
    rest = value - high
    middle = rest.astype(BF16).astype(F32)
    return high, middle, rest - middle


def pick_rows(rows, count):
    width = rows[0].shape[1]
    place = lax.broadcasted_iota(jnp.int32, (count, width), 0)
    out = jnp.zeros((count, width), F32)
    for index, row in enumerate(rows):
        out = jnp.where(place == index, row, out)
    return out


def prepare_targets(perm_ref, count_ref, sigma2_ref, xyz_ref, feat_ref, out_ref, blocks_ref):
    inv = (0.5 * LOG2E) / jnp.full((1, TILE), sigma2_ref[0], F32)
    tiles = perm_ref.shape[0]
    offset = jnp.int32(0)
    one = jnp.ones((1, TILE), F32)
    lane = lax.broadcasted_iota(jnp.int32, (1, TILE), 1)
    for tile in range(tiles):
        span = slice(tile * TILE, (tile + 1) * TILE)
        count = count_ref[perm_ref[tile]]
        xyz = xyz_ref[:, span].astype(F32)
        x0, x1, x2 = xyz[0:1], xyz[1:2], xyz[2:3]
        square = -(x0 * x0 + x1 * x1 + x2 * x2) * inv
        qh, qm, ql = split3(jnp.where(lane < count, square, MASKED))
        side = pick_rows([x0, x1, x2, one, x0, x1, x2, one, x0, x1, x2, one, qh, qm, ql], 16)
        feat = feat_ref[:, span].astype(F32)
        wide = jnp.concatenate([feat, side, jnp.zeros((48, TILE), F32), feat, feat], axis=0)
        out_ref[pl.ds(pl.multiple_of(offset, 16), TILE), :] = wide.T.astype(BF16)
        offset = offset + ((count + 15) // 16) * 16
    blank = jnp.where(lax.broadcasted_iota(jnp.int32, (ROWS, DEPTH), 1) == 76, MASKED, 0.0)
    out_ref[pl.ds(pl.multiple_of(offset, 16), ROWS), :] = blank.astype(BF16)
    blocks_ref[0] = (offset + ROWS - 1) // ROWS


def widen_sources(sigma2_ref, panel_ref, wide_ref):
    gain = SCORE_GAIN / 64 * LOG2E
    inv = (0.5 * LOG2E) / jnp.full((1, LANES), sigma2_ref[0], F32)
    one = jnp.ones((1, LANES), F32)

    def piece(index, unused):
        at = pl.ds(pl.multiple_of(index * LANES, LANES), LANES)
        both = panel_ref[index].astype(F32)
        high, middle, low = split3(both[0:64] * gain)
        y0, y1, y2 = both[64:65], both[65:66], both[66:67]
        square = -(y0 * y0 + y1 * y1 + y2 * y2) * inv
        parts = [split3(row) for row in (y0 * (2.0 * inv), y1 * (2.0 * inv), y2 * (2.0 * inv), square)]
        rows = [part[level] for level in range(3) for part in parts] + [one, one, one]
        wide_ref[0:64, at] = high.astype(BF16)
        wide_ref[64:80, at] = pick_rows(rows, 16).astype(BF16)
        wide_ref[80:128, at] = jnp.zeros((48, LANES), BF16)
        wide_ref[128:192, at] = middle.astype(BF16)
        wide_ref[192:256, at] = low.astype(BF16)
        return unused

    lax.fori_loop(0, panel_ref.shape[0], piece, 0)


def kernel_pass(blocks_ref, sigma2_ref, tgt_ref, panel_ref, kernel_ref, sum_ref, wide_ref):
    step = pl.program_id(0)

    @pl.when(step == 0)
    def _():
        widen_sources(sigma2_ref, panel_ref, wide_ref)

    def block(store):
        tgt = tgt_ref[...]
        total = jnp.zeros((ROWS, LANES), F32)
        for start in range(0, wide_ref.shape[1], 256):
            score = jnp.dot(tgt, wide_ref[:, start : start + 256], preferred_element_type=F32)
            value = jnp.exp2(score)
            rounded = value.astype(BF16)
            if store:
                kernel_ref[:, start : start + 256] = rounded
            value = rounded.astype(F32)
            total += value[:, 0:128] + value[:, 128:256]
        sum_ref[pl.ds(step, 1), :] = jnp.sum(total.T, axis=0, keepdims=True)

    blocks = blocks_ref[0]

    @pl.when((step < STORED) & (step < blocks))
    def _():
        block(True)

    @pl.when((step >= STORED) & (step < blocks))
    def _():
        block(False)


def warp_sums(acc_ref, panel_ref, anchors_ref, core_ref, out_ref, side_ref, gram_ref):
    pieces = panel_ref.shape[0]
    sources = pieces * LANES
    count = anchors_ref.shape[1]
    rate = 0.5 / ANCHOR_WIDTH * LOG2E
    one = jnp.ones((1, LANES), F32)

    def piece(index, unused):
        at = pl.ds(pl.multiple_of(index * LANES, LANES), LANES)
        y = panel_ref[index, 64:80, :].astype(F32)
        y0, y1, y2 = y[0:1], y[1:2], y[2:3]
        rh, rm, rl = split3(-(y0 * y0 + y1 * y1 + y2 * y2) * rate)
        rows = [y0, y1, y2, one, y0, y1, y2, one, y0, y1, y2, one, rh, rm, rl]
        side_ref[:, at] = pick_rows(rows, 16).astype(BF16)
        return unused

    lax.fori_loop(0, pieces, piece, 0)
    a0, a1, a2 = anchors_ref[0:1, :], anchors_ref[1:2, :], anchors_ref[2:3, :]
    square = -(a0 * a0 + a1 * a1 + a2 * a2) * rate
    parts = [split3(row) for row in (a0 * (2.0 * rate), a1 * (2.0 * rate), a2 * (2.0 * rate), square)]
    ones = jnp.ones((1, count), F32)
    rows = [part[level] for level in range(3) for part in parts] + [ones, ones, ones]
    anchor_side = pick_rows(rows, LANES).T.astype(BF16)[:, 0:16]
    sums = acc_ref[...]
    sums = sums + pltpu.roll(sums, 4, 0)
    acc_ref[...] = sums
    gram_ref[...] = jnp.zeros_like(gram_ref)
    width = 512

    def chunk(index, unused):
        at = pl.ds(pl.multiple_of(index * width, width), width)
        side = side_ref[:, at]
        basis = jnp.exp2(jnp.dot(anchor_side, side, preferred_element_type=F32))
        moment = acc_ref[:, at]
        mass = moment[3:4, :]
        pull = moment - mass * side.astype(F32)[0:8]
        left = jnp.concatenate([basis * mass, pull, jnp.zeros_like(pull)], axis=0)
        left_high = left.astype(BF16)
        left_low = (left - left_high.astype(F32)).astype(BF16)
        basis_high = basis.astype(BF16)
        basis_low = (basis - basis_high.astype(F32)).astype(BF16)
        last = (((1,), (1,)), ((), ()))
        first = lax.dot_general(
            jnp.concatenate([left_high, left_low], axis=0), basis_high, last, preferred_element_type=F32
        )
        second = lax.dot_general(left_high, basis_low, last, preferred_element_type=F32)
        gram_ref[...] += first[0:272] + first[272:544] + second
        return unused

    lax.fori_loop(0, sources // width, chunk, 0)
    total = jnp.sum(acc_ref[3:4, :])
    row = lax.broadcasted_iota(jnp.int32, (8, LANES), 0)
    core = core_ref[0]
    for half in range(2):
        at = jnp.where(core == half, 0, 1)
        if half == 0:
            out_ref[at, 0:128, :] = gram_ref[0:128, 0:128]
            out_ref[at, 128:192, :] = gram_ref[0:64, 128:256]
        else:
            out_ref[at, 0:64, :] = gram_ref[64:128, 128:256]
            out_ref[at, 64:192, :] = gram_ref[128:256, 128:256]
        pulled = gram_ref[256:264, half * LANES : (half + 1) * LANES]
        out_ref[at, 192:200, :] = jnp.where(row == 3, total, pulled)
        for r in range(32):
            s = (half * 32 + r) * LANES
            out_ref[at, 200 + r : 201 + r, :] = acc_ref[3:4, s : s + LANES]


def moment_pass(
    blocks_ref, sigma2_ref, outlier_ref, core_ref, sum_ref, tgt_ref, kernel_ref, panel_ref, anchors_ref,
    out_ref, wide_ref, acc_ref, side_ref, gram_ref, *, total_sources,
):
    step = pl.program_id(0)

    @pl.when(step == 0)
    def _():
        acc_ref[...] = jnp.zeros_like(acc_ref)

    outlier = jnp.full((1, ROWS), outlier_ref[0], F32)
    floor = outlier / (1.0 - outlier) * total_sources
    normal = jnp.sum(sum_ref[:, pl.ds(step, 1), :], axis=0) + floor
    side = tgt_ref[:, 0:128].astype(F32).T[64:72]
    weight = side / normal
    high = weight.astype(BF16).astype(F32)
    row = lax.broadcasted_iota(jnp.int32, weight.shape, 0)
    weight = jnp.where(row < 4, high, weight - high).astype(BF16)

    blocks = blocks_ref[0]

    @pl.when((step < STORED) & (step < blocks))
    def _():
        for start in range(0, kernel_ref.shape[1], 1024):
            at = slice(start, start + 1024)
            acc_ref[:, at] += jnp.dot(weight, kernel_ref[:, at], preferred_element_type=F32)

    @pl.when((step == STORED) & (step < blocks))
    def _():
        widen_sources(sigma2_ref, panel_ref, wide_ref)

    @pl.when((step >= STORED) & (step < blocks))
    def _():
        for start in range(0, wide_ref.shape[1], 512):
            at = slice(start, start + 512)
            score = jnp.dot(tgt_ref[...], wide_ref[:, at], preferred_element_type=F32)
            value = jnp.exp2(score).astype(BF16)
            acc_ref[:, at] += jnp.dot(weight, value, preferred_element_type=F32)

    @pl.when(step == blocks - 1)
    def _():
        warp_sums(acc_ref, panel_ref, anchors_ref, core_ref, out_ref, side_ref, gram_ref)


def squared_gap(first, second):
    gap_a = first[0][:, None] - second[0][None, :]
    gap_b = first[1][:, None] - second[1][None, :]
    gap_c = first[2][:, None] - second[2][None, :]
    return gap_a * gap_a + gap_b * gap_b + gap_c * gap_c


def warp_solve(basis, gram, pulled, total, anchors, sigma2, warp_lambda):
    anchor_gram = jnp.exp(-squared_gap(anchors, anchors) * (0.5 / ANCHOR_WIDTH))
    system = gram / total + warp_lambda[0] * sigma2[0] * (
        anchor_gram + jnp.eye(anchors.shape[1], dtype=F32)
    )
    factor = jnp.linalg.cholesky(system)
    coeffs = jax.scipy.linalg.cho_solve((factor, True), (pulled / total).T)
    return lax.dot_general(
        coeffs, basis, (((0,), (1,)), ((), ())),
        precision=lax.Precision.HIGHEST, preferred_element_type=F32,
    )


def gather(value, axis):
    return lax.all_gather(value, axis, axis=0, tiled=True)


def local(
    tgt_coords, tgt_embed, tile_perm, tile_count, src_coords, src_embed, anchors, sigma2,
    outlier_weight, warp_lambda,
):
    cells = tgt_coords.shape[1]
    zs, ys, cs, xs = (lax.axis_size(name) for name in ("z", "y", "c", "x"))
    pieces = zs * ys * cs
    sources = pieces * LANES
    blocks_max = cells // ROWS

    own = jnp.concatenate([src_embed, src_coords, jnp.zeros((13, LANES), BF16)], axis=0)[None]
    panel = gather(gather(gather(own, "y"), "z"), "c")

    targets, blocks = pl.pallas_call(
        prepare_targets,
        in_specs=[SCALAR, SCALAR, SCALAR, WHOLE, WHOLE],
        out_specs=[WHOLE, SCALAR],
        out_shape=[
            jax.ShapeDtypeStruct((cells + TILE, DEPTH), BF16),
            jax.ShapeDtypeStruct((1,), jnp.int32),
        ],
        name="prepare_targets",
    )(tile_perm, tile_count, sigma2, tgt_coords, tgt_embed)

    def at_block(i, b):
        return jnp.minimum(i, b[0] - 1), 0

    def at_stored(i, b):
        return jnp.minimum(jnp.minimum(i, b[0] - 1), STORED - 1), 0

    kernel, sums = pl.pallas_call(
        kernel_pass,
        grid_spec=pltpu.PrefetchScalarGridSpec(
            num_scalar_prefetch=1,
            grid=(blocks_max,),
            in_specs=[
                SCALAR,
                pl.BlockSpec((ROWS, DEPTH), at_block),
                pl.BlockSpec((pieces, 80, LANES), lambda i, b: (0, 0, 0)),
            ],
            out_specs=[
                pl.BlockSpec((ROWS, sources), at_stored),
                pl.BlockSpec((blocks_max, ROWS), lambda i, b: (0, 0)),
            ],
            scratch_shapes=[pltpu.VMEM((DEPTH, sources), BF16)],
        ),
        out_shape=[
            jax.ShapeDtypeStruct((STORED * ROWS, sources), BF16),
            jax.ShapeDtypeStruct((blocks_max, ROWS), F32),
        ],
        compiler_params=pltpu.CompilerParams(vmem_limit_bytes=40 << 20),
        name="kernel_pass",
    )(blocks, sigma2, targets, panel)

    all_sums = gather(sums[None], "x")

    core = lax.axis_index("c").astype(jnp.int32)[None]
    share = pl.pallas_call(
        functools.partial(moment_pass, total_sources=sources * xs),
        grid_spec=pltpu.PrefetchScalarGridSpec(
            num_scalar_prefetch=1,
            grid=(blocks_max,),
            in_specs=[
                SCALAR,
                SCALAR,
                SCALAR,
                pl.BlockSpec((xs, blocks_max, ROWS), lambda i, b: (0, 0, 0)),
                pl.BlockSpec((ROWS, DEPTH), at_block),
                pl.BlockSpec((ROWS, sources), at_stored),
                pl.BlockSpec((pieces, 80, LANES), lambda i, b: (0, 0, 0)),
                pl.BlockSpec((3, 256), lambda i, b: (0, 0)),
            ],
            out_specs=pl.BlockSpec((2, HALF, LANES), lambda i, b: (0, 0, 0)),
            scratch_shapes=[
                pltpu.VMEM((DEPTH, sources), BF16),
                pltpu.VMEM((8, sources), F32),
                pltpu.VMEM((16, sources), BF16),
                pltpu.VMEM((272, 256), F32),
            ],
        ),
        out_shape=jax.ShapeDtypeStruct((2, HALF, LANES), F32),
        compiler_params=pltpu.CompilerParams(vmem_limit_bytes=40 << 20),
        name="moment_pass",
    )(blocks, sigma2, outlier_weight, core, all_sums, targets, kernel, panel, anchors)

    part = share[0] + lax.ppermute(share[1], "c", [(0, 1), (1, 0)])
    part = jnp.sum(lax.all_gather(part, "y"), axis=0)
    part = jnp.sum(lax.all_gather(part, "z"), axis=0)
    warp = jnp.sum(lax.all_gather(part[:WARP_ROWS], "x"), axis=0)
    both = lax.all_gather(jnp.concatenate([warp, part[WARP_ROWS:]], axis=0), "c")

    first, second = both[0], both[1]
    upper = jnp.concatenate([first[128:192], second[0:64]], axis=0)
    gram = jnp.concatenate(
        [
            jnp.concatenate([first[0:128], upper], axis=1),
            jnp.concatenate([upper.T, second[64:192]], axis=1),
        ],
        axis=0,
    )
    pulled = jnp.concatenate([first[192:195], second[192:195]], axis=1)
    total = first[195, 0]
    masses_all = both[:, WARP_ROWS:].reshape(pieces, LANES)
    place = (lax.axis_index("c") * zs + lax.axis_index("z")) * ys + lax.axis_index("y")
    masses = lax.dynamic_slice_in_dim(masses_all, place, 1, 0)[0]

    src_xyz = src_coords.astype(F32)
    basis = jnp.exp(-squared_gap(src_xyz, anchors) * (0.5 / ANCHOR_WIDTH))
    shift = warp_solve(basis, gram, pulled, total, anchors, sigma2, warp_lambda)
    return (src_xyz + shift, masses)


def solution(mesh):
    fine = Mesh(mesh.devices.reshape(8, 4, 2, 4), ("z", "y", "c", "x"))
    tgt = ("z", "y", "c")
    both = ("z", "y", "c", "x")
    placed = (
        P(None, tgt), P(None, tgt), P(tgt), P(), P(None, both), P(None, both), P(), P(), P(), P(),
    )
    return jax.shard_map(
        local, mesh=fine, in_specs=placed, out_specs=(P(None, both), P(both)), check_vma=False
    )
```

```python
import functools
import math

import jax
import jax.numpy as jnp
from jax import lax
from jax.experimental import pallas as pl
from jax.experimental.pallas import tpu as pltpu
from jax.sharding import Mesh
from jax.sharding import PartitionSpec as P

TILE = 512
SCORE_GAIN = 4.0
ANCHOR_WIDTH = 0.1
LOG2E = math.log2(math.e)

ROWS = 256
LANES = 128
DEPTH = 256
STORED = 14
MASKED = -30000.0
GRAM_ROWS = 6

F32 = jnp.float32
BF16 = jnp.bfloat16
WHOLE = pl.BlockSpec(memory_space=pltpu.VMEM)
SCALAR = pl.BlockSpec(memory_space=pltpu.SMEM)


def split3(value):
    high = value.astype(BF16).astype(F32)
    rest = value - high
    middle = rest.astype(BF16).astype(F32)
    return high, middle, rest - middle


def pick_rows(rows, count):
    width = rows[0].shape[1]
    place = lax.broadcasted_iota(jnp.int32, (count, width), 0)
    out = jnp.zeros((count, width), F32)
    for index, row in enumerate(rows):
        out = jnp.where(place == index, row, out)
    return out


def prepare(
    perm_ref, count_ref, sigma2_ref, xyz_ref, feat_ref, src_xyz_ref, src_feat_ref,
    lots_ref, tgt_ref, blocks_ref,
):
    one = jnp.ones((1, LANES), F32)
    inv = (0.5 * LOG2E) / jnp.full((1, LANES), sigma2_ref[0], F32)
    y = src_xyz_ref[...].astype(F32)
    y = [y[c : c + 1] for c in range(3)]
    square = -(y[0] * y[0] + y[1] * y[1] + y[2] * y[2]) * inv
    side = pick_rows([*y, *y, *y, *split3(square), one, one, one], 16)
    source = jnp.concatenate([src_feat_ref[...], side.astype(BF16)], axis=0)
    for lot in range(lots_ref.shape[0]):
        lots_ref[lot] = source

    gain = SCORE_GAIN / 64 * LOG2E
    inv = (0.5 * LOG2E) / jnp.full((1, TILE), sigma2_ref[0], F32)
    one = jnp.ones((1, TILE), F32)
    lane = lax.broadcasted_iota(jnp.int32, (1, TILE), 1)
    tiles = perm_ref.shape[0]
    offset = jnp.int32(0)
    for tile in range(tiles):
        span = slice(tile * TILE, (tile + 1) * TILE)
        count = count_ref[perm_ref[tile]]
        xyz = xyz_ref[:, span].astype(F32)
        x = [xyz[c : c + 1] for c in range(3)]
        square = -(x[0] * x[0] + x[1] * x[1] + x[2] * x[2]) * inv
        parts = [split3(row * (2.0 * inv)) for row in x]
        own = split3(jnp.where(lane < count, square, MASKED))
        rows = [part[level] for level in range(3) for part in parts] + [one, one, one, *own]
        rows = rows + [jnp.zeros_like(one)] + [*x, one] * 2
        high, middle, low = split3(feat_ref[:, span].astype(F32) * gain)
        wide = jnp.concatenate(
            [high, pick_rows(rows, 24), jnp.zeros((40, TILE), F32), middle, low], axis=0
        )
        tgt_ref[pl.ds(pl.multiple_of(offset, 16), TILE), :] = wide.T.astype(BF16)
        offset = offset + ((count + 15) // 16) * 16
    blank = jnp.where(lax.broadcasted_iota(jnp.int32, (ROWS, DEPTH), 1) == 76, MASKED, 0.0)
    tgt_ref[pl.ds(pl.multiple_of(offset, 16), ROWS), :] = blank.astype(BF16)
    blocks_ref[0] = (offset + ROWS - 1) // ROWS


def widened(wide_ref, start, width):
    feat = wide_ref[0:64, start : start + width]
    return jnp.concatenate([wide_ref[:, start : start + width], feat, feat], axis=0)


def kernel_pass(blocks_ref, tgt_ref, own_ref, other_ref, kernel_ref, sum_ref, wide_ref):
    step = pl.program_id(0)

    @pl.when(step == 0)
    def _():
        wide_ref[80:128, :] = jnp.zeros((48, wide_ref.shape[1]), BF16)
        for lot, panel_ref in enumerate((own_ref, other_ref)):
            for piece in range(panel_ref.shape[0]):
                start = (lot * panel_ref.shape[0] + piece) * LANES
                wide_ref[0:80, start : start + LANES] = panel_ref[piece]

    def block(store):
        tgt = tgt_ref[...]
        total = jnp.zeros((ROWS, LANES), F32)
        for start in range(0, wide_ref.shape[1], 256):
            score = jnp.dot(tgt, widened(wide_ref, start, 256), preferred_element_type=F32)
            value = jnp.exp2(score)
            rounded = value.astype(BF16)
            if store:
                kernel_ref[:, start : start + 256] = rounded
            value = rounded.astype(F32)
            total += value[:, 0:128] + value[:, 128:256]
        sum_ref[pl.ds(step, 1), :] = jnp.sum(total.T, axis=0, keepdims=True)

    blocks = blocks_ref[0]

    @pl.when((step < STORED) & (step < blocks))
    def _():
        block(True)

    @pl.when((step >= STORED) & (step < blocks))
    def _():
        block(False)


def warp_sums(acc_ref, side_ref, anchors_ref, core_ref, out_ref, gram_ref):
    pieces = out_ref.shape[1]
    sources = side_ref.shape[1]
    count = anchors_ref.shape[1]
    rate = 0.5 / ANCHOR_WIDTH * LOG2E
    a0, a1, a2 = anchors_ref[0:1, :], anchors_ref[1:2, :], anchors_ref[2:3, :]
    square = -(a0 * a0 + a1 * a1 + a2 * a2) * rate
    parts = [split3(row * (2.0 * rate)) for row in (a0, a1, a2)]
    zero = jnp.zeros((1, count), F32)
    rows = [part[level] for level in range(3) for part in parts] + [zero] * 3 + [*split3(square)]
    anchor_side = pick_rows(rows, LANES).T.astype(BF16)[:, 0:16]
    sums = acc_ref[...]
    sums = sums + pltpu.roll(sums, 4, 0)
    acc_ref[...] = sums
    gram_ref[...] = jnp.zeros_like(gram_ref)
    width = 2048

    def chunk(index, unused):
        at = pl.ds(pl.multiple_of(index * width, width), width)
        side = side_ref[:, at]
        y = side.astype(F32)[0:8]
        y0, y1, y2 = y[0:1], y[1:2], y[2:3]
        square = (y0 * y0 + y1 * y1 + y2 * y2) * rate
        basis = jnp.exp2(jnp.dot(anchor_side, side, preferred_element_type=F32) - square)
        moment = acc_ref[:, at]
        mass = moment[3:4, :]
        pull = moment - mass * y
        left = jnp.concatenate([basis * mass, pull, jnp.zeros_like(pull)], axis=0)
        left_high = left.astype(BF16)
        left_low = (left - left_high.astype(F32)).astype(BF16)
        basis_high = basis.astype(BF16)
        basis_low = (basis - basis_high.astype(F32)).astype(BF16)
        last = (((1,), (1,)), ((), ()))
        first = lax.dot_general(
            jnp.concatenate([left_high, left_low], axis=0), basis_high, last, preferred_element_type=F32
        )
        second = lax.dot_general(left_high, basis_low, last, preferred_element_type=F32)
        gram_ref[...] += first[0:272] + first[272:544] + second
        return unused

    lax.fori_loop(0, sources // width, chunk, 0)
    total = jnp.sum(acc_ref[3:4, :])
    row = lax.broadcasted_iota(jnp.int32, (8, LANES), 0)
    core = core_ref[0]
    out_ref[:, :, GRAM_ROWS : GRAM_ROWS + 1, :] = jnp.zeros((2, pieces, 1, LANES), F32)
    for half in range(2):
        at = jnp.where(core == half, 0, 1)
        for piece in range(pieces):
            start = piece * GRAM_ROWS
            for r in range(start, start + GRAM_ROWS):
                if half == 0:
                    line = gram_ref[r : r + 1, 0:128] if r < 128 else gram_ref[r - 128 : r - 127, 128:256]
                else:
                    line = gram_ref[r + 64 : r + 65, 128:256]
                out_ref[at, piece, r - start : r - start + 1, :] = line
            s = (half * pieces + piece) * LANES
            out_ref[half, piece, 7:8, :] = acc_ref[3:4, s : s + LANES]
        pulled = gram_ref[256:264, half * LANES : (half + 1) * LANES]
        pulled = jnp.where(row == 3, total, pulled)
        for r in range(4):
            out_ref[at, r, GRAM_ROWS : GRAM_ROWS + 1, :] = pulled[r : r + 1]


def moment_pass(
    blocks_ref, outlier_ref, core_ref, sum0_ref, sum1_ref, sum2_ref, sum3_ref, tgt_ref,
    kernel_ref, side_ref, wide_hbm_ref, anchors_ref, out_ref, wide_ref, acc_ref, gram_ref, arrived, *,
    total_sources,
):
    step = pl.program_id(0)

    @pl.when(step == 0)
    def _():
        acc_ref[...] = jnp.zeros_like(acc_ref)

    outlier = jnp.full((1, ROWS), outlier_ref[0], F32)
    floor = outlier / (1.0 - outlier) * total_sources
    normal = floor
    for ref in (sum0_ref, sum1_ref, sum2_ref, sum3_ref):
        normal = normal + ref[pl.ds(step, 1), :]
    side = tgt_ref[:, 0:128].astype(F32).T[80:88]
    weight = side / normal
    high = weight.astype(BF16).astype(F32)
    row = lax.broadcasted_iota(jnp.int32, weight.shape, 0)
    weight = jnp.where(row < 4, high, weight - high).astype(BF16)

    blocks = blocks_ref[0]

    @pl.when((step < STORED) & (step < blocks))
    def _():
        for start in range(0, kernel_ref.shape[1], 1024):
            at = slice(start, start + 1024)
            acc_ref[:, at] += jnp.dot(weight, kernel_ref[:, at], preferred_element_type=F32)

    @pl.when((step == STORED) & (step < blocks))
    def _():
        copy = pltpu.make_async_copy(wide_hbm_ref, wide_ref, arrived)
        copy.start()
        copy.wait()

    @pl.when((step >= STORED) & (step < blocks))
    def _():
        for start in range(0, wide_ref.shape[1], 512):
            at = slice(start, start + 512)
            score = jnp.dot(tgt_ref[...], widened(wide_ref, start, 512), preferred_element_type=F32)
            value = jnp.exp2(score).astype(BF16)
            acc_ref[:, at] += jnp.dot(weight, value, preferred_element_type=F32)

    @pl.when(step == blocks - 1)
    def _():
        warp_sums(acc_ref, side_ref, anchors_ref, core_ref, out_ref, gram_ref)


def squared_gap(first, second):
    gap_a, gap_b, gap_c = (first[c] - second[c] for c in range(3))
    return gap_a * gap_a + gap_b * gap_b + gap_c * gap_c


def halves(value):
    high = value.astype(BF16)
    return high, (value - high.astype(F32)).astype(BF16)


def dot3(first, second):
    (a, b), (c, d) = first, second
    wide = functools.partial(jnp.dot, preferred_element_type=F32)
    return wide(a, c) + (wide(a, d) + wide(b, c))


def dot_full(first, second):
    return jnp.dot(first, second, precision=lax.Precision.HIGHEST, preferred_element_type=F32)


def warp_update(
    sigma2_ref, lambda_ref, anchors_ref, xyz_ref, mass_ref, sums_ref, out_ref, out_mass_ref,
    system_ref, inverse_ref,
):
    pieces = sums_ref.shape[1]
    count = anchors_ref.shape[1]
    for half in range(2):
        for piece in range(pieces):
            for r in range(piece * GRAM_ROWS, (piece + 1) * GRAM_ROWS):
                line = sums_ref[half, piece, r - piece * GRAM_ROWS : r - piece * GRAM_ROWS + 1, :]
                if half == 1:
                    system_ref[r + 64 : r + 65, 128:256] = line
                elif r < 128:
                    system_ref[r : r + 1, 0:128] = line
                else:
                    system_ref[r - 128 : r - 127, 128:256] = line
    system_ref[128:256, 0:128] = system_ref[0:128, 128:256].T
    pulled = [
        jnp.concatenate([sums_ref[half, r, GRAM_ROWS : GRAM_ROWS + 1, :] for half in range(2)], axis=1)
        for r in range(3)
    ]
    total = sums_ref[0, 3, GRAM_ROWS : GRAM_ROWS + 1, 0:1]
    pulled = pick_rows(pulled, 8) / total

    rows = [anchors_ref[c : c + 1, :] for c in range(3)]
    columns = jnp.concatenate([pick_rows(rows, 8), jnp.zeros((120, count), F32)], axis=0).T
    columns = [columns[:, c : c + 1] for c in range(3)]
    rate = 0.5 / ANCHOR_WIDTH
    anchor_gram = jnp.exp(-squared_gap(columns, rows) * rate)
    place = lax.broadcasted_iota(jnp.int32, (count, count), 0)
    eye = jnp.where(place == lax.broadcasted_iota(jnp.int32, (count, count), 1), 1.0, 0.0)
    weight = lambda_ref[0] * sigma2_ref[0]
    system = system_ref[...] / total + weight * (anchor_gram + eye)
    system_ref[...] = system

    low = weight
    high = jnp.max(jnp.sum(jnp.abs(system), axis=0, keepdims=True)) * 1.0001
    start = 2.0 / jnp.full((1, count), low + high, F32)
    bound = jnp.max(jnp.full((8, LANES), high - low, F32) / jnp.full((8, LANES), high + low, F32))

    def narrowed(bound):
        square = jnp.full((8, LANES), bound * bound, F32)
        return jnp.max(2.0 / (2.0 - square)), jnp.max(square / (2.0 - square))

    scale, bound = narrowed(bound)
    inverse_ref[...] = (scale * start) * (2.0 * eye - start * system)
    system_halves = halves(system)

    def improve(bound):
        scale, after = narrowed(bound)
        inverse = inverse_ref[...]
        parts = halves(inverse)
        residual = 2.0 * eye - dot3(system_halves, parts)
        inverse_ref[...] = scale * dot3(parts, halves(residual))
        return after

    lax.while_loop(lambda bound: bound > 1e-4, improve, bound)
    inverse = inverse_ref[...]
    coeffs = dot_full(pulled, inverse)
    for _ in range(3):
        coeffs = coeffs + dot_full(pulled - dot_full(coeffs, system), inverse)

    xyz = xyz_ref[...].astype(F32)
    basis = jnp.exp(-squared_gap(columns, [xyz[c : c + 1] for c in range(3)]) * rate)
    out_ref[...] = xyz + dot_full(coeffs, basis)[0:3]
    out_mass_ref[...] = mass_ref[7:8, :]


def spread(value, axes):
    lots = jnp.broadcast_to(value, (lax.axis_size(axes), *value.shape[1:]))
    return lax.all_to_all(lots, axes, 0, 0, tiled=True)


def turned(value, axis, by):
    size = lax.axis_size(axis)
    return lax.ppermute(value, axis, [(i, (i + by) % size) for i in range(size)])


def local(
    tgt_coords, tgt_embed, tile_perm, tile_count, src_coords, src_embed, anchors, sigma2,
    outlier_weight, warp_lambda,
):
    cells = tgt_coords.shape[1]
    zs, ys, cs, xs = (lax.axis_size(name) for name in ("z", "y", "c", "x"))
    pieces = zs * ys
    sources = pieces * cs * LANES
    blocks_max = cells // ROWS

    lots, targets, blocks = pl.pallas_call(
        prepare,
        in_specs=[SCALAR, SCALAR, SCALAR, WHOLE, WHOLE, WHOLE, WHOLE],
        out_specs=[WHOLE, WHOLE, SCALAR],
        out_shape=[
            jax.ShapeDtypeStruct((pieces, 80, LANES), BF16),
            jax.ShapeDtypeStruct((cells + TILE, DEPTH), BF16),
            jax.ShapeDtypeStruct((1,), jnp.int32),
        ],
        name="prepare",
    )(tile_perm, tile_count, sigma2, tgt_coords, tgt_embed, src_coords, src_embed)

    own = lax.all_to_all(lots, ("z", "y"), 0, 0, tiled=True)
    other = lax.ppermute(own, "c", [(0, 1), (1, 0)])

    def at_block(i, b):
        return jnp.minimum(i, b[0] - 1), 0

    def at_stored(i, b):
        return jnp.minimum(jnp.minimum(i, b[0] - 1), STORED - 1), 0

    kernel, sums, wide = pl.pallas_call(
        kernel_pass,
        grid_spec=pltpu.PrefetchScalarGridSpec(
            num_scalar_prefetch=1,
            grid=(blocks_max,),
            in_specs=[
                pl.BlockSpec((ROWS, DEPTH), at_block),
                pl.BlockSpec((pieces, 80, LANES), lambda i, b: (0, 0, 0)),
                pl.BlockSpec((pieces, 80, LANES), lambda i, b: (0, 0, 0)),
            ],
            out_specs=[
                pl.BlockSpec((ROWS, sources), at_stored),
                pl.BlockSpec((blocks_max, ROWS), lambda i, b: (0, 0)),
                pl.BlockSpec((DEPTH // 2, sources), lambda i, b: (0, 0)),
            ],
        ),
        out_shape=[
            jax.ShapeDtypeStruct((STORED * ROWS, sources), BF16),
            jax.ShapeDtypeStruct((blocks_max, ROWS), F32),
            jax.ShapeDtypeStruct((DEPTH // 2, sources), BF16),
        ],
        compiler_params=pltpu.CompilerParams(vmem_limit_bytes=40 << 20),
        name="kernel_pass",
    )(blocks, targets, own, other)

    all_sums = [sums] + [turned(sums, "x", by) for by in range(1, xs)]

    core = lax.axis_index("c").astype(jnp.int32)[None]
    share = pl.pallas_call(
        functools.partial(moment_pass, total_sources=sources * xs),
        grid_spec=pltpu.PrefetchScalarGridSpec(
            num_scalar_prefetch=1,
            grid=(blocks_max,),
            in_specs=[
                SCALAR,
                SCALAR,
                *[pl.BlockSpec((blocks_max, ROWS), lambda i, b: (0, 0))] * xs,
                pl.BlockSpec((ROWS, DEPTH), at_block),
                pl.BlockSpec((ROWS, sources), at_stored),
                pl.BlockSpec((16, sources), lambda i, b: (4, 0)),
                pl.BlockSpec(memory_space=pltpu.HBM),
                pl.BlockSpec((3, 256), lambda i, b: (0, 0)),
            ],
            out_specs=pl.BlockSpec((cs, pieces, 8, LANES), lambda i, b: (0, 0, 0, 0)),
            scratch_shapes=[
                pltpu.VMEM((DEPTH // 2, sources), BF16),
                pltpu.VMEM((8, sources), F32),
                pltpu.VMEM((272, 256), F32),
                pltpu.SemaphoreType.DMA,
            ],
        ),
        out_shape=jax.ShapeDtypeStruct((cs, pieces, 8, LANES), F32),
        compiler_params=pltpu.CompilerParams(vmem_limit_bytes=40 << 20),
        name="moment_pass",
    )(blocks, outlier_weight, core, *all_sums, targets, kernel, wide, wide, anchors)

    part = share[0] + lax.ppermute(share[1], "c", [(0, 1), (1, 0)])
    part = jnp.sum(lax.all_to_all(part, ("z", "y"), 0, 0, tiled=True), axis=0)
    total = part + turned(part, "x", 1) + turned(part, "x", 2) + turned(part, "x", 3)
    both = lax.all_gather(spread(total[None], ("z", "y")), "c")

    warped, masses = pl.pallas_call(
        warp_update,
        in_specs=[SCALAR, SCALAR, WHOLE, WHOLE, WHOLE, WHOLE],
        out_specs=[WHOLE, WHOLE],
        out_shape=[jax.ShapeDtypeStruct((3, LANES), F32), jax.ShapeDtypeStruct((1, LANES), F32)],
        scratch_shapes=[pltpu.VMEM((256, 256), F32)] * 2,
        name="warp_update",
    )(sigma2, warp_lambda, anchors, src_coords, part, both)
    return (warped, masses.reshape(LANES))


def solution(mesh):
    fine = Mesh(mesh.devices.reshape(8, 4, 2, 4), ("z", "y", "c", "x"))
    tgt = ("z", "y", "c")
    both = ("z", "y", "c", "x")
    placed = (
        P(None, tgt), P(None, tgt), P(tgt), P(), P(None, both), P(None, both), P(), P(), P(), P(),
    )
    return jax.shard_map(
        local, mesh=fine, in_specs=placed, out_specs=(P(None, both), P(both)), check_vma=False
    )
```

```python
import functools
import math

import jax
import jax.numpy as jnp
from jax import lax
from jax.experimental import pallas as pl
from jax.experimental.pallas import tpu as pltpu
from jax.sharding import Mesh
from jax.sharding import PartitionSpec as P

TILE = 512
SCORE_GAIN = 4.0
ANCHOR_WIDTH = 0.1
LOG2E = math.log2(math.e)

UNIT = 256
LANES = 128
DEPTH = 256
KEPT = (2, 2, 2, 2, 2, 1)
MASKED = -30000.0
GRAM_ROWS = 6

F32 = jnp.float32
BF16 = jnp.bfloat16
WHOLE = pl.BlockSpec(memory_space=pltpu.VMEM)
SCALAR = pl.BlockSpec(memory_space=pltpu.SMEM)


def split3(value):
    high = value.astype(BF16).astype(F32)
    rest = value - high
    middle = rest.astype(BF16).astype(F32)
    return high, middle, rest - middle


def pick_rows(rows, count):
    width = rows[0].shape[1]
    place = lax.broadcasted_iota(jnp.int32, (count, width), 0)
    out = jnp.zeros((count, width), F32)
    for index, row in enumerate(rows):
        out = jnp.where(place == index, row, out)
    return out


def prepare(
    core_ref, outlier_ref, sigma2_ref, perm_hbm, count_hbm, xyz_hbm, feat_hbm, src_xyz_hbm, src_feat_hbm,
    lots_ref, tgt_ref, units_ref, outlier_out_ref,
    perm_ref, count_ref, xyz_ref, feat_ref, src_xyz_ref, src_feat_ref, arrived,
):
    pairs = [
        (src_xyz_hbm, src_xyz_ref), (src_feat_hbm, src_feat_ref), (perm_hbm, perm_ref),
        (count_hbm, count_ref), (xyz_hbm, xyz_ref), (feat_hbm, feat_ref),
    ]
    copies = [pltpu.make_async_copy(*pair, arrived.at[index]) for index, pair in enumerate(pairs)]
    for copy in copies:
        copy.start()
    for copy in copies:
        copy.wait()
    one = jnp.ones((1, LANES), F32)
    inv = (0.5 * LOG2E) / jnp.full((1, LANES), sigma2_ref[0], F32)
    y = src_xyz_ref[...].astype(F32)
    y = [y[c : c + 1] for c in range(3)]
    square = -(y[0] * y[0] + y[1] * y[1] + y[2] * y[2]) * inv
    side = pick_rows([*y, *y, *y, *split3(square), one, one, one], 16)
    source = jnp.concatenate([src_feat_ref[...], side.astype(BF16)], axis=0)
    for lot in range(lots_ref.shape[0]):
        lots_ref[lot] = source

    gain = SCORE_GAIN / 64 * LOG2E
    inv = (0.5 * LOG2E) / jnp.full((1, TILE), sigma2_ref[0], F32)
    one = jnp.ones((1, TILE), F32)
    lane = lax.broadcasted_iota(jnp.int32, (1, TILE), 1)
    tiles = perm_ref.shape[0]
    offset = jnp.int32(0)
    for tile in range(tiles):
        span = slice(tile * TILE, (tile + 1) * TILE)
        count = count_ref[perm_ref[tile]]
        xyz = xyz_ref[:, span].astype(F32)
        x = [xyz[c : c + 1] for c in range(3)]
        square = -(x[0] * x[0] + x[1] * x[1] + x[2] * x[2]) * inv
        parts = [split3(row * (2.0 * inv)) for row in x]
        own = split3(jnp.where(lane < count, square, MASKED))
        rows = [part[level] for level in range(3) for part in parts] + [one, one, one, *own]
        rows = rows + [jnp.zeros_like(one)] + [*x, one] * 2
        high, middle, low = split3(feat_ref[:, span].astype(F32) * gain)
        wide = jnp.concatenate(
            [high, pick_rows(rows, 24), jnp.zeros((40, TILE), F32), middle, low], axis=0
        )
        tgt_ref[pl.ds(pl.multiple_of(offset, 16), TILE), :] = wide.T.astype(BF16)
        offset = offset + ((count + 15) // 16) * 16
    blank = jnp.where(lax.broadcasted_iota(jnp.int32, (UNIT, DEPTH), 1) == 76, MASKED, 0.0)
    tgt_ref[pl.ds(pl.multiple_of(offset, 16), UNIT), :] = blank.astype(BF16)
    units_ref[0] = (offset + UNIT - 1) // UNIT
    units_ref[1] = core_ref[0]
    outlier_out_ref[0] = outlier_ref[0]


def widened(wide_ref, start, width):
    feat = wide_ref[0:64, start : start + width]
    return jnp.concatenate([wide_ref[:, start : start + width], feat, feat], axis=0)


def kernel_pass(units_ref, tgt_ref, own_ref, other_ref, *refs):
    *kernel_refs, sum_ref, wide_ref = refs
    sources = wide_ref.shape[1]
    wide_ref[80:128, :] = jnp.zeros((48, sources), BF16)
    for lot, panel_ref in enumerate((own_ref, other_ref)):
        for piece in range(panel_ref.shape[0]):
            start = (lot * panel_ref.shape[0] + piece) * LANES
            wide_ref[0:80, start : start + LANES] = panel_ref[piece]

    def block(unit, count, kernel_ref=None, first=0):
        tgt = tgt_ref[unit_rows(unit, count), :]
        total = jnp.zeros((count * UNIT, LANES), F32)
        for start in range(0, sources, 256):
            score = jnp.dot(tgt, widened(wide_ref, start, 256), preferred_element_type=F32)
            rounded = jnp.exp2(score).astype(BF16)
            if kernel_ref is not None:
                kernel_ref[unit_rows(unit - first, count), start : start + 256] = rounded
            value = rounded.astype(F32)
            total += value[:, 0:128] + value[:, 128:256]
        for part in range(count):
            lines = total[part * UNIT : (part + 1) * UNIT]
            sum_ref[pl.ds(unit + part, 1), :] = jnp.sum(lines.T, axis=0, keepdims=True)

    each_unit(units_ref[0], kernel_refs, block)


def unit_rows(unit, count):
    return pl.ds(pl.multiple_of(unit * UNIT, UNIT), count * UNIT)


def each_unit(units, kernel_refs, block):
    for index, kernel_ref in enumerate(kernel_refs):
        first = sum(KEPT[:index])
        here = jnp.clip(units - first, 0, KEPT[index])

        def two(step, unused, first=first, kernel_ref=kernel_ref):
            block(first + step * 2, 2, kernel_ref, first)
            return unused

        lax.fori_loop(0, here // 2, two, 0)

        @pl.when(here % 2 == 1)
        def _(first=first, here=here, kernel_ref=kernel_ref):
            block(first + here - 1, 1, kernel_ref, first)

    def beyond(unit, unused):
        block(unit, 1)
        return unused

    lax.fori_loop(sum(KEPT), units, beyond, 0)


def warp_sums(acc_ref, wide_ref, anchors_ref, core, out_ref, gram_ref):
    pieces = out_ref.shape[1]
    sources = wide_ref.shape[1]
    count = anchors_ref.shape[1]
    rate = 0.5 / ANCHOR_WIDTH * LOG2E
    a0, a1, a2 = anchors_ref[0:1, :], anchors_ref[1:2, :], anchors_ref[2:3, :]
    square = -(a0 * a0 + a1 * a1 + a2 * a2) * rate
    parts = [split3(row * (2.0 * rate)) for row in (a0, a1, a2)]
    zero = jnp.zeros((1, count), F32)
    rows = [part[level] for level in range(3) for part in parts] + [zero] * 3 + [*split3(square)]
    anchor_side = pick_rows(rows, LANES).T.astype(BF16)[:, 0:16]
    sums = acc_ref[...]
    sums = sums + pltpu.roll(sums, 4, 0)
    acc_ref[...] = sums
    gram_ref[...] = jnp.zeros_like(gram_ref)
    width = 1024

    def chunk(index, unused):
        at = pl.ds(pl.multiple_of(index * width, width), width)
        side = wide_ref[64:80, at]
        y = side.astype(F32)[0:8]
        y0, y1, y2 = y[0:1], y[1:2], y[2:3]
        square = (y0 * y0 + y1 * y1 + y2 * y2) * rate
        basis = jnp.exp2(jnp.dot(anchor_side, side, preferred_element_type=F32) - square)
        moment = acc_ref[:, at]
        mass = moment[3:4, :]
        pull = moment - mass * y
        left = jnp.concatenate([basis * mass, pull, jnp.zeros_like(pull)], axis=0)
        left_high = left.astype(BF16)
        left_low = (left - left_high.astype(F32)).astype(BF16)
        basis_high = basis.astype(BF16)
        basis_low = (basis - basis_high.astype(F32)).astype(BF16)
        last = (((1,), (1,)), ((), ()))
        first = lax.dot_general(
            jnp.concatenate([left_high, left_low], axis=0), basis_high, last, preferred_element_type=F32
        )
        second = lax.dot_general(left_high, basis_low, last, preferred_element_type=F32)
        gram_ref[...] += first[0:272] + first[272:544] + second
        return unused

    lax.fori_loop(0, sources // width, chunk, 0)
    total = jnp.sum(acc_ref[3:4, :])
    row = lax.broadcasted_iota(jnp.int32, (8, LANES), 0)
    out_ref[:, :, GRAM_ROWS : GRAM_ROWS + 1, :] = jnp.zeros((2, pieces, 1, LANES), F32)
    for half in range(2):
        at = jnp.where(core == half, 0, 1)
        for piece in range(pieces):
            start = piece * GRAM_ROWS
            for r in range(start, start + GRAM_ROWS):
                if half == 0:
                    line = gram_ref[r : r + 1, 0:128] if r < 128 else gram_ref[r - 128 : r - 127, 128:256]
                else:
                    line = gram_ref[r + 64 : r + 65, 128:256]
                out_ref[at, piece, r - start : r - start + 1, :] = line
            s = (half * pieces + piece) * LANES
            out_ref[half, piece, 7:8, :] = acc_ref[3:4, s : s + LANES]
        pulled = gram_ref[256:264, half * LANES : (half + 1) * LANES]
        pulled = jnp.where(row == 3, total, pulled)
        for r in range(4):
            out_ref[at, r, GRAM_ROWS : GRAM_ROWS + 1, :] = pulled[r : r + 1]


def moment_pass(
    units_ref, outlier_ref, sum0_ref, sum1_ref, sum2_ref, sum3_ref, tgt_ref, wide_ref, anchors_ref,
    *refs, total_sources,
):
    *kernel_refs, out_ref, acc_ref, gram_ref, part_ref = refs
    sources = wide_ref.shape[1]
    outlier = jnp.full((1, UNIT), outlier_ref[0], F32)
    floor = outlier / (1.0 - outlier) * total_sources
    acc_ref[...] = jnp.zeros_like(acc_ref)

    def block(unit, count, kernel_ref=None, first=0):
        normals = []
        for part in range(count):
            normal = floor
            for ref in (sum0_ref, sum1_ref, sum2_ref, sum3_ref):
                normal = normal + ref[pl.ds(unit + part, 1), :]
            normals.append(normal)
        side = tgt_ref[unit_rows(unit, count), 0:128].astype(F32).T[80:88]
        weight = side / jnp.concatenate(normals, axis=1)
        high = weight.astype(BF16).astype(F32)
        row = lax.broadcasted_iota(jnp.int32, weight.shape, 0)
        weight = jnp.where(row < 4, high, weight - high).astype(BF16)
        if kernel_ref is not None:
            for start in range(0, sources, 1024):
                at = slice(start, start + 1024)
                value = kernel_ref[unit_rows(unit - first, count), at]
                acc_ref[:, at] += jnp.dot(weight, value, preferred_element_type=F32)
            return
        width = part_ref.shape[1]
        for first in range(0, sources, width):
            for start in range(0, width, 256):
                wide = widened(wide_ref, first + start, 256)
                score = jnp.dot(tgt_ref[unit_rows(unit, count), :], wide, preferred_element_type=F32)
                part_ref[:, start : start + 256] = jnp.exp2(score).astype(BF16)
            for start in range(0, width, 1024):
                at = slice(first + start, first + start + 1024)
                value = part_ref[:, start : start + 1024]
                acc_ref[:, at] += jnp.dot(weight, value, preferred_element_type=F32)

    each_unit(units_ref[0], kernel_refs, block)
    warp_sums(acc_ref, wide_ref, anchors_ref, units_ref[1], out_ref, gram_ref)


def squared_gap(first, second):
    gap_a, gap_b, gap_c = (first[c] - second[c] for c in range(3))
    return gap_a * gap_a + gap_b * gap_b + gap_c * gap_c


def halves(value):
    high = value.astype(BF16)
    return high, (value - high.astype(F32)).astype(BF16)


def dot3(first, second):
    (a, b), (c, d) = first, second
    wide = functools.partial(jnp.dot, preferred_element_type=F32)
    return wide(a, c) + (wide(a, d) + wide(b, c))


def dot_full(first, second):
    return jnp.dot(first, second, precision=lax.Precision.HIGHEST, preferred_element_type=F32)


def warp_update(
    sigma2_ref, lambda_ref, anchors_ref, xyz_ref, mass_ref, sums_ref, out_ref, out_mass_ref,
    system_ref, inverse_ref,
):
    pieces = sums_ref.shape[1]
    count = anchors_ref.shape[1]
    for half in range(2):
        for piece in range(pieces):
            for r in range(piece * GRAM_ROWS, (piece + 1) * GRAM_ROWS):
                line = sums_ref[half, piece, r - piece * GRAM_ROWS : r - piece * GRAM_ROWS + 1, :]
                if half == 1:
                    system_ref[r + 64 : r + 65, 128:256] = line
                elif r < 128:
                    system_ref[r : r + 1, 0:128] = line
                else:
                    system_ref[r - 128 : r - 127, 128:256] = line
    system_ref[128:256, 0:128] = system_ref[0:128, 128:256].T
    pulled = [
        jnp.concatenate([sums_ref[half, r, GRAM_ROWS : GRAM_ROWS + 1, :] for half in range(2)], axis=1)
        for r in range(3)
    ]
    total = sums_ref[0, 3, GRAM_ROWS : GRAM_ROWS + 1, 0:1]
    pulled = pick_rows(pulled, 8) / total

    rows = [anchors_ref[c : c + 1, :] for c in range(3)]
    columns = jnp.concatenate([pick_rows(rows, 8), jnp.zeros((120, count), F32)], axis=0).T
    columns = [columns[:, c : c + 1] for c in range(3)]
    rate = 0.5 / ANCHOR_WIDTH
    anchor_gram = jnp.exp(-squared_gap(columns, rows) * rate)
    place = lax.broadcasted_iota(jnp.int32, (count, count), 0)
    eye = jnp.where(place == lax.broadcasted_iota(jnp.int32, (count, count), 1), 1.0, 0.0)
    weight = lambda_ref[0] * sigma2_ref[0]
    system = system_ref[...] / total + weight * (anchor_gram + eye)
    system_ref[...] = system

    low = weight
    high = jnp.max(jnp.sum(jnp.abs(system), axis=0, keepdims=True)) * 1.0001
    start = 2.0 / jnp.full((1, count), low + high, F32)
    bound = jnp.max(jnp.full((8, LANES), high - low, F32) / jnp.full((8, LANES), high + low, F32))

    def narrowed(bound):
        square = jnp.full((8, LANES), bound * bound, F32)
        return jnp.max(2.0 / (2.0 - square)), jnp.max(square / (2.0 - square))

    scale, bound = narrowed(bound)
    inverse_ref[...] = (scale * start) * (2.0 * eye - start * system)
    system_halves = halves(system)

    def improve(bound):
        scale, after = narrowed(bound)
        inverse = inverse_ref[...]
        parts = halves(inverse)
        residual = 2.0 * eye - dot3(system_halves, parts)
        inverse_ref[...] = scale * dot3(parts, halves(residual))
        return after

    lax.while_loop(lambda bound: bound > 1e-4, improve, bound)
    inverse = inverse_ref[...]
    coeffs = dot_full(pulled, inverse)
    for _ in range(3):
        coeffs = coeffs + dot_full(pulled - dot_full(coeffs, system), inverse)

    xyz = xyz_ref[...].astype(F32)
    basis = jnp.exp(-squared_gap(columns, [xyz[c : c + 1] for c in range(3)]) * rate)
    out_ref[...] = xyz + dot_full(coeffs, basis)[0:3]
    out_mass_ref[...] = mass_ref[7:8, :]


def spread(value, axes):
    lots = jnp.broadcast_to(value, (lax.axis_size(axes), *value.shape[1:]))
    return lax.all_to_all(lots, axes, 0, 0, tiled=True)


def turned(value, axis, by):
    size = lax.axis_size(axis)
    return lax.ppermute(value, axis, [(i, (i + by) % size) for i in range(size)])


def local(
    tgt_coords, tgt_embed, tile_perm, tile_count, src_coords, src_embed, anchors, sigma2,
    outlier_weight, warp_lambda,
):
    cells = tgt_coords.shape[1]
    zs, ys, cs, xs = (lax.axis_size(name) for name in ("z", "y", "c", "x"))
    pieces = zs * ys
    sources = pieces * cs * LANES

    core = lax.axis_index("c").astype(jnp.int32)[None]
    inputs = (tile_perm, tile_count, tgt_coords, tgt_embed, src_coords, src_embed)
    inputs = [pltpu.with_memory_space_constraint(value, pltpu.HBM) for value in inputs]
    lots, targets, units, outlier = pl.pallas_call(
        prepare,
        in_specs=[SCALAR] * 3 + [pl.BlockSpec(memory_space=pltpu.HBM)] * len(inputs),
        out_specs=[WHOLE, WHOLE, SCALAR, SCALAR],
        out_shape=[
            jax.ShapeDtypeStruct((pieces, 80, LANES), BF16),
            jax.ShapeDtypeStruct((cells + TILE, DEPTH), BF16),
            jax.ShapeDtypeStruct((2,), jnp.int32),
            jax.ShapeDtypeStruct((1,), F32),
        ],
        scratch_shapes=[
            *[pltpu.SMEM(value.shape, value.dtype) for value in inputs[:2]],
            *[pltpu.VMEM(value.shape, value.dtype) for value in inputs[2:]],
            pltpu.SemaphoreType.DMA((len(inputs),)),
        ],
        compiler_params=pltpu.CompilerParams(vmem_limit_bytes=8 << 20),
        name="prepare",
    )(core, outlier_weight, sigma2, *inputs)

    own = lax.all_to_all(lots, ("z", "y"), 0, 0, tiled=True)
    other = lax.ppermute(own, "c", [(0, 1), (1, 0)])

    *kernels, sums, wide = pl.pallas_call(
        kernel_pass,
        in_specs=[SCALAR, WHOLE, WHOLE, WHOLE],
        out_specs=[WHOLE] * (len(KEPT) + 2),
        out_shape=[
            *[jax.ShapeDtypeStruct((count * UNIT, sources), BF16) for count in KEPT],
            jax.ShapeDtypeStruct((cells // UNIT, UNIT), F32),
            jax.ShapeDtypeStruct((DEPTH // 2, sources), BF16),
        ],
        compiler_params=pltpu.CompilerParams(vmem_limit_bytes=2 << 20),
        name="kernel_pass",
    )(units, targets, own, other)

    all_sums = [sums] + [turned(sums, "x", by) for by in range(1, xs)]

    share = pl.pallas_call(
        functools.partial(moment_pass, total_sources=sources * xs),
        in_specs=[SCALAR, SCALAR, *[WHOLE] * (xs + 3 + len(KEPT))],
        out_specs=WHOLE,
        out_shape=jax.ShapeDtypeStruct((cs, pieces, 8, LANES), F32),
        scratch_shapes=[
            pltpu.VMEM((8, sources), F32),
            pltpu.VMEM((272, 256), F32),
            pltpu.VMEM((UNIT, sources // 4), BF16),
        ],
        compiler_params=pltpu.CompilerParams(vmem_limit_bytes=5 << 20),
        name="moment_pass",
    )(units, outlier, *all_sums, targets, wide, anchors, *kernels)

    part = share[0] + lax.ppermute(share[1], "c", [(0, 1), (1, 0)])
    part = jnp.sum(lax.all_to_all(part, ("z", "y"), 0, 0, tiled=True), axis=0)
    total = part + turned(part, "x", 1) + turned(part, "x", 2) + turned(part, "x", 3)
    both = lax.all_gather(spread(total[None], ("z", "y")), "c")

    warped, masses = pl.pallas_call(
        warp_update,
        in_specs=[SCALAR, SCALAR, WHOLE, WHOLE, WHOLE, WHOLE],
        out_specs=[WHOLE, WHOLE],
        out_shape=[jax.ShapeDtypeStruct((3, LANES), F32), jax.ShapeDtypeStruct((1, LANES), F32)],
        scratch_shapes=[pltpu.VMEM((256, 256), F32)] * 2,
        compiler_params=pltpu.CompilerParams(vmem_limit_bytes=6 << 20),
        name="warp_update",
    )(sigma2, warp_lambda, anchors, src_coords, part, both)
    return (warped, masses.reshape(LANES))


def solution(mesh):
    fine = Mesh(mesh.devices.reshape(8, 4, 2, 4), ("z", "y", "c", "x"))
    tgt = ("z", "y", "c")
    both = ("z", "y", "c", "x")
    placed = (
        P(None, tgt), P(None, tgt), P(tgt), P(), P(None, both), P(None, both), P(), P(), P(), P(),
    )
    return jax.shard_map(
        local, mesh=fine, in_specs=placed, out_specs=(P(None, both), P(both)), check_vma=False
    )
```

```python
import functools
import math

import jax
import jax.numpy as jnp
from jax import lax
from jax.experimental import pallas as pl
from jax.experimental.pallas import tpu as pltpu
from jax.sharding import Mesh
from jax.sharding import PartitionSpec as P

TILE = 512
SCORE_GAIN = 4.0
ANCHOR_WIDTH = 0.1
LOG2E = math.log2(math.e)

UNIT = 256
LANES = 128
GROUP = 2048
DEPTH = 256
KEPT = (2, 2, 2, 2, 2, 1)
MASKED = -30000.0
GRAM_ROWS = 6

F32 = jnp.float32
BF16 = jnp.bfloat16
WHOLE = pl.BlockSpec(memory_space=pltpu.VMEM)
SCALAR = pl.BlockSpec(memory_space=pltpu.SMEM)


def split3(value):
    high = value.astype(BF16).astype(F32)
    rest = value - high
    middle = rest.astype(BF16).astype(F32)
    return high, middle, rest - middle


def pick_rows(rows, count):
    width = rows[0].shape[1]
    place = lax.broadcasted_iota(jnp.int32, (count, width), 0)
    out = jnp.zeros((count, width), F32)
    for index, row in enumerate(rows):
        out = jnp.where(place == index, row, out)
    return out


def prepare(
    core_ref, outlier_ref, sigma2_ref, perm_hbm, count_hbm, xyz_hbm, feat_hbm, src_xyz_hbm, src_feat_hbm,
    lots_ref, tgt_ref, units_ref, outlier_out_ref,
    perm_ref, count_ref, xyz_ref, feat_ref, src_xyz_ref, src_feat_ref, arrived,
):
    pairs = [
        (src_xyz_hbm, src_xyz_ref), (src_feat_hbm, src_feat_ref), (perm_hbm, perm_ref),
        (count_hbm, count_ref), (xyz_hbm, xyz_ref), (feat_hbm, feat_ref),
    ]
    copies = [pltpu.make_async_copy(*pair, arrived.at[index]) for index, pair in enumerate(pairs)]
    for copy in copies:
        copy.start()
    for copy in copies:
        copy.wait()
    one = jnp.ones((1, LANES), F32)
    inv = (0.5 * LOG2E) / jnp.full((1, LANES), sigma2_ref[0], F32)
    y = src_xyz_ref[...].astype(F32)
    y = [y[c : c + 1] for c in range(3)]
    square = -(y[0] * y[0] + y[1] * y[1] + y[2] * y[2]) * inv
    side = pick_rows([*y, *y, *y, *split3(square), one, one, one], 16)
    source = jnp.concatenate([src_feat_ref[...], side.astype(BF16)], axis=0)
    for lot in range(lots_ref.shape[0]):
        lots_ref[lot] = source

    gain = SCORE_GAIN / 64 * LOG2E
    inv = (0.5 * LOG2E) / jnp.full((1, TILE), sigma2_ref[0], F32)
    one = jnp.ones((1, TILE), F32)
    lane = lax.broadcasted_iota(jnp.int32, (1, TILE), 1)
    tiles = perm_ref.shape[0]
    offset = jnp.int32(0)
    for tile in range(tiles):
        span = slice(tile * TILE, (tile + 1) * TILE)
        count = count_ref[perm_ref[tile]]
        xyz = xyz_ref[:, span].astype(F32)
        x = [xyz[c : c + 1] for c in range(3)]
        square = -(x[0] * x[0] + x[1] * x[1] + x[2] * x[2]) * inv
        parts = [split3(row * (2.0 * inv)) for row in x]
        own = split3(jnp.where(lane < count, square, MASKED))
        rows = [part[level] for level in range(3) for part in parts] + [one, one, one, *own]
        rows = rows + [jnp.zeros_like(one)] + [*x, one] * 2
        high, middle, low = split3(feat_ref[:, span].astype(F32) * gain)
        wide = jnp.concatenate(
            [high, pick_rows(rows, 24), jnp.zeros((40, TILE), F32), middle, low], axis=0
        )
        tgt_ref[pl.ds(pl.multiple_of(offset, 16), TILE), :] = wide.T.astype(BF16)
        offset = offset + ((count + 15) // 16) * 16
    blank = jnp.where(lax.broadcasted_iota(jnp.int32, (UNIT, DEPTH), 1) == 76, MASKED, 0.0)
    tgt_ref[pl.ds(pl.multiple_of(offset, 16), UNIT), :] = blank.astype(BF16)
    units_ref[0] = (offset + UNIT - 1) // UNIT
    units_ref[1] = core_ref[0]
    outlier_out_ref[0] = outlier_ref[0]


def widened(wide_ref, group, start):
    at = slice(start, start + 256)
    feat = wide_ref[group, 0:64, at]
    return jnp.concatenate([wide_ref[group, :, at], feat, feat], axis=0)


def kernel_pass(units_ref, tgt_ref, own_ref, other_ref, *refs):
    *kernel_refs, sum_ref, wide_ref, total_ref = refs
    groups = wide_ref.shape[0]
    wide_ref[:, 80:128, :] = jnp.zeros((groups, 48, GROUP), BF16)
    for lot, panel_ref in enumerate((own_ref, other_ref)):
        for piece in range(panel_ref.shape[0]):
            group, start = divmod((lot * panel_ref.shape[0] + piece) * LANES, GROUP)
            wide_ref[group, 0:80, start : start + LANES] = panel_ref[piece]

    def block(unit, count, kernel_ref=None, row=0):
        height = count * UNIT
        total_ref[0:height, :] = jnp.zeros((height, LANES), F32)

        def columns(group, unused):
            tgt = tgt_ref[unit_rows(unit, count), :]
            total = jnp.zeros((height, LANES), F32)
            for start in range(0, GROUP, 256):
                score = jnp.dot(tgt, widened(wide_ref, group, start), preferred_element_type=F32)
                rounded = jnp.exp2(score).astype(BF16)
                if kernel_ref is not None:
                    kernel_ref[group, row : row + height, start : start + 256] = rounded
                value = rounded.astype(F32)
                total += value[:, 0:128] + value[:, 128:256]
            total_ref[0:height, :] += total
            return unused

        lax.fori_loop(0, groups, columns, 0)
        for part in range(count):
            lines = total_ref[part * UNIT : (part + 1) * UNIT, :]
            sum_ref[pl.ds(unit + part, 1), :] = jnp.sum(lines.T, axis=0, keepdims=True)

    each_unit(units_ref[0], kernel_refs, block)


def unit_rows(unit, count):
    start = unit * UNIT
    return pl.ds(start if isinstance(unit, int) else pl.multiple_of(start, UNIT), count * UNIT)


def each_unit(units, kernel_refs, block):
    for index, kernel_ref in enumerate(kernel_refs):
        first = sum(KEPT[:index])
        if KEPT[index] == 2:
            pl.when(units >= first + 2)(functools.partial(block, first, 2, kernel_ref))
        pl.when(units == first + 1)(functools.partial(block, first, 1, kernel_ref))
    if KEPT[-1] == 1:
        pl.when(units > sum(KEPT))(functools.partial(block, sum(KEPT) - 1, 1, kernel_refs[-1]))

    def beyond(unit, unused):
        block(unit, 1)
        return unused

    lax.fori_loop(sum(KEPT), units, beyond, 0)


def warp_sums(acc_ref, wide_ref, anchors_ref, core, out_ref, gram_ref):
    pieces = out_ref.shape[1] // 8
    groups = wide_ref.shape[0]
    count = anchors_ref.shape[1]
    rate = 0.5 / ANCHOR_WIDTH * LOG2E
    a0, a1, a2 = anchors_ref[0:1, :], anchors_ref[1:2, :], anchors_ref[2:3, :]
    square = -(a0 * a0 + a1 * a1 + a2 * a2) * rate
    parts = [split3(row * (2.0 * rate)) for row in (a0, a1, a2)]
    zero = jnp.zeros((1, count), F32)
    rows = [part[level] for level in range(3) for part in parts] + [zero] * 3 + [*split3(square)]
    anchor_side = pick_rows(rows, LANES).T.astype(BF16)[:, 0:16]
    sums = acc_ref[...]
    sums = sums + pltpu.roll(sums, 4, 0)
    acc_ref[...] = sums
    gram_ref[...] = jnp.zeros_like(gram_ref)
    width = GROUP // 2

    def chunk(index, unused):
        at = pl.ds(pl.multiple_of(index * width, width), width)
        half = pl.ds(pl.multiple_of(index % 2 * width, width), width)
        side = wide_ref[index // 2, 64:80, half]
        y = side.astype(F32)[0:8]
        y0, y1, y2 = y[0:1], y[1:2], y[2:3]
        square = (y0 * y0 + y1 * y1 + y2 * y2) * rate
        basis = jnp.exp2(jnp.dot(anchor_side, side, preferred_element_type=F32) - square)
        moment = acc_ref[:, at]
        mass = moment[3:4, :]
        pull = moment - mass * y
        root = jnp.sqrt(mass)
        pull = pull * lax.rsqrt(jnp.maximum(mass, 1e-36))
        scaled = basis * root
        scaled_high, scaled_low = halves(scaled)
        pull_high, pull_low = halves(jnp.concatenate([pull, jnp.zeros_like(pull)], axis=0))
        last = (((1,), (1,)), ((), ()))
        left = jnp.concatenate([scaled_high, pull_high, pull_low], axis=0)
        first = lax.dot_general(left, scaled_high, last, preferred_element_type=F32)
        second = lax.dot_general(left[0:272], scaled_low, last, preferred_element_type=F32)
        gram_ref[0:288, :] += first
        gram_ref[288:560, :] += second
        return unused

    lax.fori_loop(0, groups * 2, chunk, 0)
    cross = gram_ref[288:544, :]
    gram_ref[0:256, :] += cross + cross.T
    total = jnp.sum(acc_ref[3:4, :])
    row = lax.broadcasted_iota(jnp.int32, (8, LANES), 0)
    for half in range(2):
        at = jnp.where(core == half, 0, 1)
        for r in range(GRAM_ROWS):
            out_ref[at, pl.ds(r, pieces, stride=8), :] = gram_ref[gram_place(half, r, pieces)]
        out_ref[at, pl.ds(GRAM_ROWS, pieces, stride=8), :] = jnp.zeros((pieces, LANES), F32)
        lanes = slice(half * LANES, (half + 1) * LANES)
        pulled = gram_ref[256:264, lanes] + gram_ref[272:280, lanes] + gram_ref[544:552, lanes]
        pulled = jnp.where(row == 3, total, pulled)
        for r in range(4):
            out_ref[at, r * 8 + GRAM_ROWS : r * 8 + GRAM_ROWS + 1, :] = pulled[r : r + 1]
        for piece in range(pieces):
            s = (half * pieces + piece) * LANES
            out_ref[half, piece * 8 + 7 : piece * 8 + 8, :] = acc_ref[3:4, s : s + LANES]


def gram_place(half, r, pieces):
    if half == 0:
        first, right = (r * pieces, 0) if r < 4 else ((r - 4) * pieces, 1)
    else:
        first, right = 64 + r * pieces, 1
    return slice(first, first + pieces), slice(right * LANES, (right + 1) * LANES)


def moment_pass(
    units_ref, outlier_ref, sum0_ref, sum1_ref, sum2_ref, sum3_ref, tgt_ref, wide_ref, anchors_ref,
    *refs, total_sources,
):
    *kernel_refs, out_ref, acc_ref, gram_ref, part_ref = refs
    groups = wide_ref.shape[0]
    outlier = jnp.full((1, UNIT), outlier_ref[0], F32)
    floor = outlier / (1.0 - outlier) * total_sources
    acc_ref[...] = jnp.zeros_like(acc_ref)

    def block(unit, count, kernel_ref=None):
        normals = []
        for part in range(count):
            normal = floor
            for ref in (sum0_ref, sum1_ref, sum2_ref, sum3_ref):
                normal = normal + ref[pl.ds(unit + part, 1), :]
            normals.append(normal)
        side = tgt_ref[unit_rows(unit, count), 0:128].astype(F32).T[80:88]
        weight = side / jnp.concatenate(normals, axis=1)
        high = weight.astype(BF16).astype(F32)
        row = lax.broadcasted_iota(jnp.int32, weight.shape, 0)
        weight = jnp.where(row < 4, high, weight - high).astype(BF16)
        for group in range(groups):
            if kernel_ref is None:
                for start in range(0, GROUP, 256):
                    tgt = tgt_ref[unit_rows(unit, count), :]
                    score = jnp.dot(tgt, widened(wide_ref, group, start), preferred_element_type=F32)
                    part_ref[:, start : start + 256] = jnp.exp2(score).astype(BF16)
            for start in range(0, GROUP, 1024):
                at = slice(group * GROUP + start, group * GROUP + start + 1024)
                if kernel_ref is None:
                    value = part_ref[:, start : start + 1024]
                else:
                    value = kernel_ref[group, 0 : count * UNIT, start : start + 1024]
                acc_ref[:, at] += jnp.dot(weight, value, preferred_element_type=F32)

    each_unit(units_ref[0], kernel_refs, block)
    warp_sums(acc_ref, wide_ref, anchors_ref, units_ref[1], out_ref, gram_ref)


def squared_gap(first, second):
    gap_a, gap_b, gap_c = (first[c] - second[c] for c in range(3))
    return gap_a * gap_a + gap_b * gap_b + gap_c * gap_c


def halves(value):
    high = value.astype(BF16)
    return high, (value - high.astype(F32)).astype(BF16)


def dot3(first, second):
    (a, b), (c, d) = first, second
    wide = functools.partial(jnp.dot, preferred_element_type=F32)
    return wide(a, c) + (wide(a, d) + wide(b, c))


def dot_full(first, second):
    return jnp.dot(first, second, precision=lax.Precision.HIGHEST, preferred_element_type=F32)


def warp_update(
    sigma2_ref, lambda_ref, anchors_ref, xyz_ref, mass_ref, sums_ref, out_ref, out_mass_ref,
    system_ref, inverse_ref,
):
    pieces = sums_ref.shape[1] // 8
    count = anchors_ref.shape[1]
    for half in range(2):
        for r in range(GRAM_ROWS):
            system_ref[gram_place(half, r, pieces)] = sums_ref[half, pl.ds(r, pieces, stride=8), :]
    system_ref[128:256, 0:128] = system_ref[0:128, 128:256].T
    pulled = [
        jnp.concatenate([sums_ref[half, r * 8 + GRAM_ROWS : r * 8 + GRAM_ROWS + 1, :] for half in range(2)], axis=1)
        for r in range(3)
    ]
    total = sums_ref[0, 24 + GRAM_ROWS : 25 + GRAM_ROWS, 0:1]
    pulled = pick_rows(pulled, 8) / total

    rows = [anchors_ref[c : c + 1, :] for c in range(3)]
    columns = jnp.concatenate([pick_rows(rows, 8), jnp.zeros((120, count), F32)], axis=0).T
    columns = [columns[:, c : c + 1] for c in range(3)]
    rate = 0.5 / ANCHOR_WIDTH
    anchor_gram = jnp.exp(-squared_gap(columns, rows) * rate)
    place = lax.broadcasted_iota(jnp.int32, (count, count), 0)
    eye = jnp.where(place == lax.broadcasted_iota(jnp.int32, (count, count), 1), 1.0, 0.0)
    weight = lambda_ref[0] * sigma2_ref[0]
    system = system_ref[...] / total + weight * (anchor_gram + eye)
    system_ref[...] = system

    low = weight
    high = jnp.max(jnp.sum(jnp.abs(system), axis=0, keepdims=True)) * 1.0001
    start = 2.0 / jnp.full((1, count), low + high, F32)
    bound = jnp.max(jnp.full((8, LANES), high - low, F32) / jnp.full((8, LANES), high + low, F32))

    def narrowed(bound):
        square = jnp.full((8, LANES), bound * bound, F32)
        return jnp.max(2.0 / (2.0 - square)), jnp.max(square / (2.0 - square))

    scale, bound = narrowed(bound)
    inverse_ref[...] = (scale * start) * (2.0 * eye - start * system)
    system_halves = halves(system)

    def improve(bound):
        scale, after = narrowed(bound)
        inverse = inverse_ref[...]
        parts = halves(inverse)
        residual = 2.0 * eye - dot3(system_halves, parts)
        inverse_ref[...] = scale * dot3(parts, halves(residual))
        return after

    lax.while_loop(lambda bound: bound > 1e-2, improve, bound)
    inverse = inverse_ref[...]
    coeffs = dot_full(pulled, inverse)
    for _ in range(3):
        coeffs = coeffs + dot_full(pulled - dot_full(coeffs, system), inverse)

    xyz = xyz_ref[...].astype(F32)
    basis = jnp.exp(-squared_gap(columns, [xyz[c : c + 1] for c in range(3)]) * rate)
    out_ref[...] = xyz + dot_full(coeffs, basis)[0:3]
    out_mass_ref[...] = mass_ref[7:8, :]


def spread(value, axes):
    lots = jnp.broadcast_to(value, (lax.axis_size(axes), *value.shape[1:]))
    return lax.all_to_all(lots, axes, 0, 0, tiled=True)


def turned(value, axis, by):
    size = lax.axis_size(axis)
    return lax.ppermute(value, axis, [(i, (i + by) % size) for i in range(size)])


def local(
    tgt_coords, tgt_embed, tile_perm, tile_count, src_coords, src_embed, anchors, sigma2,
    outlier_weight, warp_lambda,
):
    cells = tgt_coords.shape[1]
    zs, ys, cs, xs = (lax.axis_size(name) for name in ("z", "y", "c", "x"))
    pieces = zs * ys
    sources = pieces * cs * LANES
    groups = sources // GROUP

    core = lax.axis_index("c").astype(jnp.int32)[None]
    inputs = (tile_perm, tile_count, tgt_coords, tgt_embed, src_coords, src_embed)
    inputs = [pltpu.with_memory_space_constraint(value, pltpu.HBM) for value in inputs]
    lots, targets, units, outlier = pl.pallas_call(
        prepare,
        in_specs=[SCALAR] * 3 + [pl.BlockSpec(memory_space=pltpu.HBM)] * len(inputs),
        out_specs=[WHOLE, WHOLE, SCALAR, SCALAR],
        out_shape=[
            jax.ShapeDtypeStruct((pieces, 80, LANES), BF16),
            jax.ShapeDtypeStruct((cells + TILE, DEPTH), BF16),
            jax.ShapeDtypeStruct((2,), jnp.int32),
            jax.ShapeDtypeStruct((1,), F32),
        ],
        scratch_shapes=[
            *[pltpu.SMEM(value.shape, value.dtype) for value in inputs[:2]],
            *[pltpu.VMEM(value.shape, value.dtype) for value in inputs[2:]],
            pltpu.SemaphoreType.DMA((len(inputs),)),
        ],
        compiler_params=pltpu.CompilerParams(vmem_limit_bytes=8 << 20),
        name="prepare",
    )(core, outlier_weight, sigma2, *inputs)

    own = lax.all_to_all(lots, ("z", "y"), 0, 0, tiled=True)
    other = lax.ppermute(own, "c", [(0, 1), (1, 0)])

    *kernels, sums, wide = pl.pallas_call(
        kernel_pass,
        in_specs=[SCALAR, WHOLE, WHOLE, WHOLE],
        out_specs=[WHOLE] * (len(KEPT) + 2),
        out_shape=[
            *[jax.ShapeDtypeStruct((groups, count * UNIT, GROUP), BF16) for count in KEPT],
            jax.ShapeDtypeStruct((cells // UNIT, UNIT), F32),
            jax.ShapeDtypeStruct((groups, DEPTH // 2, GROUP), BF16),
        ],
        scratch_shapes=[pltpu.VMEM((2 * UNIT, LANES), F32)],
        compiler_params=pltpu.CompilerParams(vmem_limit_bytes=2 << 20),
        name="kernel_pass",
    )(units, targets, own, other)

    all_sums = [sums] + [turned(sums, "x", by) for by in range(1, xs)]

    share = pl.pallas_call(
        functools.partial(moment_pass, total_sources=sources * xs),
        in_specs=[SCALAR, SCALAR, *[WHOLE] * (xs + 3 + len(KEPT))],
        out_specs=WHOLE,
        out_shape=jax.ShapeDtypeStruct((cs, pieces * 8, LANES), F32),
        scratch_shapes=[
            pltpu.VMEM((8, sources), F32),
            pltpu.VMEM((560, 256), F32),
            pltpu.VMEM((UNIT, GROUP), BF16),
        ],
        compiler_params=pltpu.CompilerParams(vmem_limit_bytes=5 << 20),
        name="moment_pass",
    )(units, outlier, *all_sums, targets, wide, anchors, *kernels)

    part = share[0] + lax.ppermute(share[1], "c", [(0, 1), (1, 0)])
    part = part.reshape(pieces, 8, LANES)
    part = jnp.sum(lax.all_to_all(part, ("z", "y"), 0, 0, tiled=True), axis=0)
    total = part + turned(part, "x", 1) + turned(part, "x", 2) + turned(part, "x", 3)
    both = lax.all_gather(spread(total[None], ("z", "y")).reshape(pieces * 8, LANES), "c")

    warped, masses = pl.pallas_call(
        warp_update,
        in_specs=[SCALAR, SCALAR, WHOLE, WHOLE, WHOLE, WHOLE],
        out_specs=[WHOLE, WHOLE],
        out_shape=[jax.ShapeDtypeStruct((3, LANES), F32), jax.ShapeDtypeStruct((1, LANES), F32)],
        scratch_shapes=[pltpu.VMEM((256, 256), F32)] * 2,
        compiler_params=pltpu.CompilerParams(vmem_limit_bytes=6 << 20),
        name="warp_update",
    )(sigma2, warp_lambda, anchors, src_coords, part, both)
    return (warped, masses.reshape(LANES))


def solution(mesh):
    fine = Mesh(mesh.devices.reshape(8, 4, 2, 4), ("z", "y", "c", "x"))
    tgt = ("z", "y", "c")
    both = ("z", "y", "c", "x")
    placed = (
        P(None, tgt), P(None, tgt), P(tgt), P(), P(None, both), P(None, both), P(), P(), P(), P(),
    )
    return jax.shard_map(
        local, mesh=fine, in_specs=placed, out_specs=(P(None, both), P(both)), check_vma=False
    )
```

```python
import functools
import math

import jax
import jax.numpy as jnp
from jax import lax
from jax.experimental import pallas as pl
from jax.experimental.pallas import tpu as pltpu
from jax.sharding import Mesh
from jax.sharding import PartitionSpec as P

TILE = 512
SCORE_GAIN = 4.0
ANCHOR_WIDTH = 0.1
LOG2E = math.log2(math.e)

UNIT = 256
LANES = 128
GROUP = 2048
DEPTH = 256
KEPT = (2, 2, 2, 2, 2, 1)
MASKED = -30000.0
GRAM_ROWS = 6

F32 = jnp.float32
BF16 = jnp.bfloat16
WHOLE = pl.BlockSpec(memory_space=pltpu.VMEM)
SCALAR = pl.BlockSpec(memory_space=pltpu.SMEM)


def split3(value):
    high = value.astype(BF16).astype(F32)
    rest = value - high
    middle = rest.astype(BF16).astype(F32)
    return high, middle, rest - middle


def pick_rows(rows, count):
    width = rows[0].shape[1]
    place = lax.broadcasted_iota(jnp.int32, (count, width), 0)
    out = jnp.zeros((count, width), F32)
    for index, row in enumerate(rows):
        out = jnp.where(place == index, row, out)
    return out


def prepare(
    core_ref, outlier_ref, sigma2_ref, perm_hbm, count_hbm, xyz_hbm, feat_hbm, src_xyz_hbm, src_feat_hbm,
    lots_ref, tgt_ref, units_ref, outlier_out_ref,
    perm_ref, count_ref, xyz_ref, feat_ref, src_xyz_ref, src_feat_ref, arrived,
):
    pairs = [
        (src_xyz_hbm, src_xyz_ref), (src_feat_hbm, src_feat_ref), (perm_hbm, perm_ref),
        (count_hbm, count_ref), (xyz_hbm, xyz_ref), (feat_hbm, feat_ref),
    ]
    copies = [pltpu.make_async_copy(*pair, arrived.at[index]) for index, pair in enumerate(pairs)]
    for copy in copies:
        copy.start()
    for copy in copies[:2]:
        copy.wait()
    one = jnp.ones((1, LANES), F32)
    inv = (0.5 * LOG2E) / jnp.full((1, LANES), sigma2_ref[0], F32)
    y = src_xyz_ref[...].astype(F32)
    y = [y[c : c + 1] for c in range(3)]
    square = -(y[0] * y[0] + y[1] * y[1] + y[2] * y[2]) * inv
    side = pick_rows([*y, *y, *y, *split3(square), one, one, one], 16)
    source = jnp.concatenate([src_feat_ref[...], side.astype(BF16)], axis=0)
    for lot in range(lots_ref.shape[0]):
        lots_ref[lot] = source

    for copy in copies[2:]:
        copy.wait()
    gain = SCORE_GAIN / 64 * LOG2E
    inv = (0.5 * LOG2E) / jnp.full((1, TILE), sigma2_ref[0], F32)
    one = jnp.ones((1, TILE), F32)
    lane = lax.broadcasted_iota(jnp.int32, (1, TILE), 1)
    tiles = perm_ref.shape[0]
    offset = jnp.int32(0)
    for tile in range(tiles):
        span = slice(tile * TILE, (tile + 1) * TILE)
        count = count_ref[perm_ref[tile]]
        xyz = xyz_ref[:, span].astype(F32)
        x = [xyz[c : c + 1] for c in range(3)]
        square = -(x[0] * x[0] + x[1] * x[1] + x[2] * x[2]) * inv
        parts = [split3(row * (2.0 * inv)) for row in x]
        own = split3(jnp.where(lane < count, square, MASKED))
        rows = [part[level] for level in range(3) for part in parts] + [one, one, one, *own]
        rows = rows + [jnp.zeros_like(one)] + [*x, one] * 2
        high, middle, low = split3(feat_ref[:, span].astype(F32) * gain)
        wide = jnp.concatenate(
            [high, pick_rows(rows, 24), jnp.zeros((40, TILE), F32), middle, low], axis=0
        )
        tgt_ref[pl.ds(pl.multiple_of(offset, 16), TILE), :] = wide.T.astype(BF16)
        offset = offset + ((count + 15) // 16) * 16
    blank = jnp.where(lax.broadcasted_iota(jnp.int32, (UNIT, DEPTH), 1) == 76, MASKED, 0.0)
    tgt_ref[pl.ds(pl.multiple_of(offset, 16), UNIT), :] = blank.astype(BF16)
    units_ref[0] = (offset + UNIT - 1) // UNIT
    units_ref[1] = core_ref[0]
    outlier_out_ref[0] = outlier_ref[0]


def widened(wide_ref, group, start):
    at = slice(start, start + 256)
    feat = wide_ref[group, 0:64, at]
    return jnp.concatenate([wide_ref[group, :, at], feat, feat], axis=0)


def kernel_pass(units_ref, tgt_ref, own_ref, other_ref, *refs):
    *kernel_refs, sum_ref, wide_ref, total_ref = refs
    groups = wide_ref.shape[0]
    wide_ref[:, 80:128, :] = jnp.zeros((groups, 48, GROUP), BF16)
    for lot, panel_ref in enumerate((own_ref, other_ref)):
        for piece in range(panel_ref.shape[0]):
            group, start = divmod((lot * panel_ref.shape[0] + piece) * LANES, GROUP)
            wide_ref[group, 0:80, start : start + LANES] = panel_ref[piece]

    def block(unit, count, kernel_ref=None, row=0):
        height = count * UNIT
        total_ref[0:height, :] = jnp.zeros((height, LANES), F32)

        def columns(group, unused):
            tgt = tgt_ref[unit_rows(unit, count), :]
            total = jnp.zeros((height, LANES), F32)
            for start in range(0, GROUP, 256):
                score = jnp.dot(tgt, widened(wide_ref, group, start), preferred_element_type=F32)
                rounded = jnp.exp2(score).astype(BF16)
                if kernel_ref is not None:
                    kernel_ref[group, row : row + height, start : start + 256] = rounded
                if kernel_ref is None:
                    value = rounded.astype(F32)
                    total += value[:, 0:128] + value[:, 128:256]
            if kernel_ref is not None:
                for part in range(0, height, 16):
                    lines = kernel_ref[group, row + part : row + part + 16, :].astype(F32)
                    line = lines[:, 0:128]
                    for start in range(128, GROUP, 128):
                        line += lines[:, start : start + 128]
                    total_ref[part : part + 16, :] += line
            else:
                total_ref[0:height, :] += total
            return unused

        lax.fori_loop(0, groups, columns, 0)
        for part in range(count):
            lines = total_ref[part * UNIT : (part + 1) * UNIT, :]
            sum_ref[pl.ds(unit + part, 1), :] = jnp.sum(lines.T, axis=0, keepdims=True)

    each_unit(units_ref[0], kernel_refs, block)


def unit_rows(unit, count):
    start = unit * UNIT
    return pl.ds(start if isinstance(unit, int) else pl.multiple_of(start, UNIT), count * UNIT)


def each_unit(units, kernel_refs, block):
    for index, kernel_ref in enumerate(kernel_refs):
        first = sum(KEPT[:index])
        if KEPT[index] == 2:
            pl.when(units >= first + 2)(functools.partial(block, first, 2, kernel_ref))
        pl.when(units == first + 1)(functools.partial(block, first, 1, kernel_ref))
    if KEPT[-1] == 1:
        pl.when(units > sum(KEPT))(functools.partial(block, sum(KEPT) - 1, 1, kernel_refs[-1]))

    def beyond(unit, unused):
        block(unit, 1)
        return unused

    lax.fori_loop(sum(KEPT), units, beyond, 0)


def warp_sums(acc_ref, wide_ref, anchors_ref, core, out_ref, gram_ref):
    pieces = out_ref.shape[1] // 8
    groups = wide_ref.shape[0]
    count = anchors_ref.shape[1]
    rate = 0.5 / ANCHOR_WIDTH * LOG2E
    a0, a1, a2 = anchors_ref[0:1, :], anchors_ref[1:2, :], anchors_ref[2:3, :]
    square = -(a0 * a0 + a1 * a1 + a2 * a2) * rate
    parts = [split3(row * (2.0 * rate)) for row in (a0, a1, a2)]
    zero = jnp.zeros((1, count), F32)
    rows = [part[level] for level in range(3) for part in parts] + [zero] * 3 + [*split3(square)]
    anchor_side = pick_rows(rows, LANES).T.astype(BF16)[:, 0:16]
    sums = acc_ref[...]
    sums = sums + pltpu.roll(sums, 4, 0)
    acc_ref[...] = sums
    gram_ref[...] = jnp.zeros_like(gram_ref)
    width = GROUP // 2

    def chunk(index, unused):
        at = pl.ds(pl.multiple_of(index * width, width), width)
        half = pl.ds(pl.multiple_of(index % 2 * width, width), width)
        side = wide_ref[index // 2, 64:80, half]
        y = side.astype(F32)[0:8]
        y0, y1, y2 = y[0:1], y[1:2], y[2:3]
        square = (y0 * y0 + y1 * y1 + y2 * y2) * rate
        basis = jnp.exp2(jnp.dot(anchor_side, side, preferred_element_type=F32) - square)
        moment = acc_ref[:, at]
        mass = moment[3:4, :]
        pull = moment - mass * y
        root = jnp.sqrt(mass)
        pull = pull * lax.rsqrt(jnp.maximum(mass, 1e-36))
        scaled = basis * root
        scaled_high, scaled_low = halves(scaled)
        pull_high, pull_low = halves(jnp.concatenate([pull, jnp.zeros_like(pull)], axis=0))
        last = (((1,), (1,)), ((), ()))
        left = jnp.concatenate([scaled_high, pull_high, pull_low], axis=0)
        first = lax.dot_general(left, scaled_high, last, preferred_element_type=F32)
        second = lax.dot_general(left[0:272], scaled_low, last, preferred_element_type=F32)
        gram_ref[0:288, :] += first
        gram_ref[288:560, :] += second
        return unused

    def pair(index, unused):
        chunk(index * 2, unused)
        chunk(index * 2 + 1, unused)
        return unused

    lax.fori_loop(0, groups, pair, 0)
    cross = gram_ref[288:544, :]
    gram_ref[0:256, :] += cross + cross.T
    total = jnp.sum(acc_ref[3:4, :])
    row = lax.broadcasted_iota(jnp.int32, (8, LANES), 0)
    for half in range(2):
        at = jnp.where(core == half, 0, 1)
        for r in range(GRAM_ROWS):
            out_ref[at, pl.ds(r, pieces, stride=8), :] = gram_ref[gram_place(half, r, pieces)]
        out_ref[at, pl.ds(GRAM_ROWS, pieces, stride=8), :] = jnp.zeros((pieces, LANES), F32)
        lanes = slice(half * LANES, (half + 1) * LANES)
        pulled = gram_ref[256:264, lanes] + gram_ref[272:280, lanes] + gram_ref[544:552, lanes]
        pulled = jnp.where(row == 3, total, pulled)
        for r in range(4):
            out_ref[at, r * 8 + GRAM_ROWS : r * 8 + GRAM_ROWS + 1, :] = pulled[r : r + 1]
        for piece in range(pieces):
            s = (half * pieces + piece) * LANES
            out_ref[half, piece * 8 + 7 : piece * 8 + 8, :] = acc_ref[3:4, s : s + LANES]


def gram_place(half, r, pieces):
    if half == 0:
        first, right = (r * pieces, 0) if r < 4 else ((r - 4) * pieces, 1)
    else:
        first, right = 64 + r * pieces, 1
    return slice(first, first + pieces), slice(right * LANES, (right + 1) * LANES)


def moment_pass(
    units_ref, outlier_ref, sum0_ref, sum1_ref, sum2_ref, sum3_ref, tgt_ref, wide_ref, anchors_hbm,
    *refs, total_sources,
):
    *kernel_refs, out_ref, acc_ref, gram_ref, part_ref, anchors_ref, arrived = refs
    copy = pltpu.make_async_copy(anchors_hbm, anchors_ref, arrived)
    copy.start()
    groups = wide_ref.shape[0]
    outlier = jnp.full((1, UNIT), outlier_ref[0], F32)
    floor = outlier / (1.0 - outlier) * total_sources
    acc_ref[...] = jnp.zeros_like(acc_ref)

    def block(unit, count, kernel_ref=None):
        normals = []
        for part in range(count):
            normal = floor
            for ref in (sum0_ref, sum1_ref, sum2_ref, sum3_ref):
                normal = normal + ref[pl.ds(unit + part, 1), :]
            normals.append(normal)
        side = tgt_ref[unit_rows(unit, count), 0:128].astype(F32).T[80:88]
        weight = side / jnp.concatenate(normals, axis=1)
        high = weight.astype(BF16).astype(F32)
        row = lax.broadcasted_iota(jnp.int32, weight.shape, 0)
        weight = jnp.where(row < 4, high, weight - high).astype(BF16)
        for group in range(groups):
            if kernel_ref is None:
                for start in range(0, GROUP, 256):
                    tgt = tgt_ref[unit_rows(unit, count), :]
                    score = jnp.dot(tgt, widened(wide_ref, group, start), preferred_element_type=F32)
                    part_ref[:, start : start + 256] = jnp.exp2(score).astype(BF16)
            for start in range(0, GROUP, 1024):
                at = slice(group * GROUP + start, group * GROUP + start + 1024)
                if kernel_ref is None:
                    value = part_ref[:, start : start + 1024]
                else:
                    value = kernel_ref[group, 0 : count * UNIT, start : start + 1024]
                acc_ref[:, at] += jnp.dot(weight, value, preferred_element_type=F32)

    each_unit(units_ref[0], kernel_refs, block)
    copy.wait()
    warp_sums(acc_ref, wide_ref, anchors_ref, units_ref[1], out_ref, gram_ref)


def squared_gap(first, second):
    gap_a, gap_b, gap_c = (first[c] - second[c] for c in range(3))
    return gap_a * gap_a + gap_b * gap_b + gap_c * gap_c


def halves(value):
    high = value.astype(BF16)
    return high, (value - high.astype(F32)).astype(BF16)


def dot3(first, second):
    (a, b), (c, d) = first, second
    wide = functools.partial(jnp.dot, preferred_element_type=F32)
    return wide(a, c) + (wide(a, d) + wide(b, c))


def dot_full(first, second):
    return jnp.dot(first, second, precision=lax.Precision.HIGHEST, preferred_element_type=F32)


def warp_update(
    sigma2_ref, lambda_ref, anchors_ref, xyz_ref, mass_ref, sums_ref, out_ref, out_mass_ref,
    system_ref, inverse_ref,
):
    pieces = sums_ref.shape[1] // 8
    count = anchors_ref.shape[1]
    for half in range(2):
        for r in range(GRAM_ROWS):
            system_ref[gram_place(half, r, pieces)] = sums_ref[half, pl.ds(r, pieces, stride=8), :]
    system_ref[128:256, 0:128] = system_ref[0:128, 128:256].T
    pulled = [
        jnp.concatenate([sums_ref[half, r * 8 + GRAM_ROWS : r * 8 + GRAM_ROWS + 1, :] for half in range(2)], axis=1)
        for r in range(3)
    ]
    total = sums_ref[0, 24 + GRAM_ROWS : 25 + GRAM_ROWS, 0:1]
    pulled = pick_rows(pulled, 8) / total

    rows = [anchors_ref[c : c + 1, :] for c in range(3)]
    columns = jnp.concatenate([pick_rows(rows, 8), jnp.zeros((120, count), F32)], axis=0).T
    columns = [columns[:, c : c + 1] for c in range(3)]
    rate = 0.5 / ANCHOR_WIDTH
    anchor_gram = jnp.exp(-squared_gap(columns, rows) * rate)
    place = lax.broadcasted_iota(jnp.int32, (count, count), 0)
    eye = jnp.where(place == lax.broadcasted_iota(jnp.int32, (count, count), 1), 1.0, 0.0)
    weight = lambda_ref[0] * sigma2_ref[0]
    system = system_ref[...] / total + weight * (anchor_gram + eye)
    system_ref[...] = system

    low = weight
    high = jnp.max(jnp.sum(jnp.abs(system), axis=0, keepdims=True)) * 1.0001
    start = 2.0 / jnp.full((1, count), low + high, F32)
    bound = jnp.max(jnp.full((8, LANES), high - low, F32) / jnp.full((8, LANES), high + low, F32))

    def narrowed(bound):
        square = jnp.full((8, LANES), bound * bound, F32)
        return jnp.max(2.0 / (2.0 - square)), jnp.max(square / (2.0 - square))

    scale, bound = narrowed(bound)
    inverse_ref[...] = (scale * start) * (2.0 * eye - start * system)
    system_halves = halves(system)

    def improve(bound):
        scale, after = narrowed(bound)
        inverse = inverse_ref[...]
        parts = halves(inverse)
        residual = 2.0 * eye - dot3(system_halves, parts)
        inverse_ref[...] = scale * dot3(parts, halves(residual))
        return after

    lax.while_loop(lambda bound: bound > 1e-2, improve, bound)
    inverse = inverse_ref[...]
    coeffs = dot_full(pulled, inverse)
    for _ in range(3):
        coeffs = coeffs + dot_full(pulled - dot_full(coeffs, system), inverse)

    xyz = xyz_ref[...].astype(F32)
    basis = jnp.exp(-squared_gap(columns, [xyz[c : c + 1] for c in range(3)]) * rate)
    out_ref[...] = xyz + dot_full(coeffs, basis)[0:3]
    out_mass_ref[...] = mass_ref[7:8, :]


def spread(value, axes):
    lots = jnp.broadcast_to(value, (lax.axis_size(axes), *value.shape[1:]))
    return lax.all_to_all(lots, axes, 0, 0, tiled=True)


def turned(value, axis, by):
    size = lax.axis_size(axis)
    return lax.ppermute(value, axis, [(i, (i + by) % size) for i in range(size)])


def local(
    tgt_coords, tgt_embed, tile_perm, tile_count, src_coords, src_embed, anchors, sigma2,
    outlier_weight, warp_lambda,
):
    cells = tgt_coords.shape[1]
    zs, ys, cs, xs = (lax.axis_size(name) for name in ("z", "y", "c", "x"))
    pieces = zs * ys
    sources = pieces * cs * LANES
    groups = sources // GROUP

    core = lax.axis_index("c").astype(jnp.int32)[None]
    inputs = (tile_perm, tile_count, tgt_coords, tgt_embed, src_coords, src_embed)
    inputs = [pltpu.with_memory_space_constraint(value, pltpu.HBM) for value in inputs]
    lots, targets, units, outlier = pl.pallas_call(
        prepare,
        in_specs=[SCALAR] * 3 + [pl.BlockSpec(memory_space=pltpu.HBM)] * len(inputs),
        out_specs=[WHOLE, WHOLE, SCALAR, SCALAR],
        out_shape=[
            jax.ShapeDtypeStruct((pieces, 80, LANES), BF16),
            jax.ShapeDtypeStruct((cells + UNIT, DEPTH), BF16),
            jax.ShapeDtypeStruct((2,), jnp.int32),
            jax.ShapeDtypeStruct((1,), F32),
        ],
        scratch_shapes=[
            *[pltpu.SMEM(value.shape, value.dtype) for value in inputs[:2]],
            *[pltpu.VMEM(value.shape, value.dtype) for value in inputs[2:]],
            pltpu.SemaphoreType.DMA((len(inputs),)),
        ],
        compiler_params=pltpu.CompilerParams(vmem_limit_bytes=8 << 20),
        name="prepare",
    )(core, outlier_weight, sigma2, *inputs)

    own = lax.all_to_all(lots, ("z", "y"), 0, 0, tiled=True)
    other = lax.ppermute(own, "c", [(0, 1), (1, 0)])

    *kernels, sums, wide = pl.pallas_call(
        kernel_pass,
        in_specs=[SCALAR, WHOLE, WHOLE, WHOLE],
        out_specs=[WHOLE] * (len(KEPT) + 2),
        out_shape=[
            *[jax.ShapeDtypeStruct((groups, count * UNIT, GROUP), BF16) for count in KEPT],
            jax.ShapeDtypeStruct((cells // UNIT, UNIT), F32),
            jax.ShapeDtypeStruct((groups, DEPTH // 2, GROUP), BF16),
        ],
        scratch_shapes=[pltpu.VMEM((2 * UNIT, LANES), F32)],
        compiler_params=pltpu.CompilerParams(vmem_limit_bytes=2 << 20),
        name="kernel_pass",
    )(units, targets, own, other)

    all_sums = [sums] + [turned(sums, "x", by) for by in range(1, xs)]

    share = pl.pallas_call(
        functools.partial(moment_pass, total_sources=sources * xs),
        in_specs=[SCALAR, SCALAR, *[WHOLE] * (xs + 2), pl.BlockSpec(memory_space=pltpu.HBM), *[WHOLE] * len(KEPT)],
        out_specs=WHOLE,
        out_shape=jax.ShapeDtypeStruct((cs, pieces * 8, LANES), F32),
        scratch_shapes=[
            pltpu.VMEM((8, sources), F32),
            pltpu.VMEM((560, 256), F32),
            pltpu.VMEM((UNIT, GROUP), BF16),
            pltpu.VMEM((3, 256), F32),
            pltpu.SemaphoreType.DMA,
        ],
        compiler_params=pltpu.CompilerParams(vmem_limit_bytes=5 << 20),
        name="moment_pass",
    )(units, outlier, *all_sums, targets, wide, pltpu.with_memory_space_constraint(anchors, pltpu.HBM), *kernels)

    part = share[0] + lax.ppermute(share[1], "c", [(0, 1), (1, 0)])
    part = part.reshape(pieces, 8, LANES)
    part = jnp.sum(lax.all_to_all(part, ("z", "y"), 0, 0, tiled=True), axis=0)
    total = part + turned(part, "x", 1) + turned(part, "x", 2) + turned(part, "x", 3)
    both = lax.all_gather(spread(total[None], ("z", "y")).reshape(pieces * 8, LANES), "c")

    warped, masses = pl.pallas_call(
        warp_update,
        in_specs=[SCALAR, SCALAR, WHOLE, WHOLE, WHOLE, WHOLE],
        out_specs=[WHOLE, WHOLE],
        out_shape=[jax.ShapeDtypeStruct((3, LANES), F32), jax.ShapeDtypeStruct((1, LANES), F32)],
        scratch_shapes=[pltpu.VMEM((256, 256), F32)] * 2,
        compiler_params=pltpu.CompilerParams(vmem_limit_bytes=6 << 20),
        name="warp_update",
    )(sigma2, warp_lambda, anchors, src_coords, part, both)
    return (warped, masses.reshape(LANES))


def solution(mesh):
    fine = Mesh(mesh.devices.reshape(8, 4, 2, 4), ("z", "y", "c", "x"))
    tgt = ("z", "y", "c")
    both = ("z", "y", "c", "x")
    placed = (
        P(None, tgt), P(None, tgt), P(tgt), P(), P(None, both), P(None, both), P(), P(), P(), P(),
    )
    return jax.shard_map(
        local, mesh=fine, in_specs=placed, out_specs=(P(None, both), P(both)), check_vma=False
    )
```

```python
import functools
import math

import jax
import jax.numpy as jnp
from jax import lax
from jax.experimental import pallas as pl
from jax.experimental.pallas import tpu as pltpu
from jax.sharding import Mesh
from jax.sharding import PartitionSpec as P

TILE = 512
SCORE_GAIN = 4.0
ANCHOR_WIDTH = 0.1
LOG2E = math.log2(math.e)

UNIT = 256
LANES = 128
GROUP = 2048
DEPTH = 256
KEPT = (2, 2, 2, 2, 2, 1)
MASKED = -30000.0
GRAM_ROWS = 6

F32 = jnp.float32
BF16 = jnp.bfloat16
WHOLE = pl.BlockSpec(memory_space=pltpu.VMEM)
SCALAR = pl.BlockSpec(memory_space=pltpu.SMEM)


def split3(value):
    high = value.astype(BF16).astype(F32)
    rest = value - high
    middle = rest.astype(BF16).astype(F32)
    return high, middle, rest - middle


def pick_rows(rows, count):
    width = rows[0].shape[1]
    place = lax.broadcasted_iota(jnp.int32, (count, width), 0)
    out = jnp.zeros((count, width), F32)
    for index, row in enumerate(rows):
        out = jnp.where(place == index, row, out)
    return out


def prepare(
    core_ref, outlier_ref, sigma2_ref, src_xyz_hbm, src_feat_hbm, count_hbm, perm_hbm, xyz_hbm, feat_hbm,
    other_perm_hbm, other_xyz_hbm, other_feat_hbm, lots_ref, tgt_ref, units_ref, outlier_out_ref,
    src_xyz_ref, src_feat_ref, count_ref, perm_ref, xyz_ref, feat_ref, offset_ref, arrived,
):
    core = core_ref[0]
    pairs = [
        (src_xyz_hbm, src_xyz_ref), (src_feat_hbm, src_feat_ref), (count_hbm, count_ref),
        (perm_hbm, perm_ref.at[core]), (other_perm_hbm, perm_ref.at[1 - core]),
        (xyz_hbm, xyz_ref.at[core]), (other_xyz_hbm, xyz_ref.at[1 - core]),
        (feat_hbm, feat_ref.at[core]), (other_feat_hbm, feat_ref.at[1 - core]),
    ]
    copies = [pltpu.make_async_copy(*pair, arrived.at[index]) for index, pair in enumerate(pairs)]
    for copy in copies:
        copy.start()
    for copy in copies[:2]:
        copy.wait()
    one = jnp.ones((1, LANES), F32)
    inv = (0.5 * LOG2E) / jnp.full((1, LANES), sigma2_ref[0], F32)
    y = src_xyz_ref[...].astype(F32)
    y = [y[c : c + 1] for c in range(3)]
    square = -(y[0] * y[0] + y[1] * y[1] + y[2] * y[2]) * inv
    side = pick_rows([*y, *y, *y, *split3(square), one, one, one], 16)
    source = jnp.concatenate([src_feat_ref[...], side.astype(BF16)], axis=0)
    for lot in range(lots_ref.shape[0]):
        lots_ref[lot] = source

    for copy in copies[2:]:
        copy.wait()
    gain = SCORE_GAIN / 64 * LOG2E
    inv = (0.5 * LOG2E) / jnp.full((1, TILE), sigma2_ref[0], F32)
    one = jnp.ones((1, TILE), F32)
    lane = lax.broadcasted_iota(jnp.int32, (1, TILE), 1)

    tiles = perm_ref.shape[1]
    offset = jnp.int32(0)
    for tile in range(2 * tiles):
        offset_ref[tile] = offset
        count = count_ref[perm_ref[tile // tiles, tile % tiles]]
        offset = offset + ((count + 15) // 16) * 16
    offset_ref[2 * tiles] = offset
    split = jnp.int32(tiles)
    least = jnp.maximum(offset_ref[tiles], offset - offset_ref[tiles])
    for tile in range(1, 2 * tiles):
        most = jnp.maximum(offset_ref[tile], offset - offset_ref[tile])
        split = jnp.where(most < least, tile, split)
        least = jnp.minimum(most, least)
    first = jnp.where(core == 0, 0, split)
    last = jnp.where(core == 0, split, 2 * tiles)
    base = offset_ref[first]

    def place(tile, unused):
        half = (tile >= tiles).astype(jnp.int32)
        slot = tile - half * tiles
        span = pl.ds(pl.multiple_of(slot * TILE, TILE), TILE)
        count = count_ref[perm_ref[half, slot]]
        xyz = xyz_ref[half, :, span].astype(F32)
        x = [xyz[c : c + 1] for c in range(3)]
        square = -(x[0] * x[0] + x[1] * x[1] + x[2] * x[2]) * inv
        parts = [split3(row * (2.0 * inv)) for row in x]
        own = split3(jnp.where(lane < count, square, MASKED))
        rows = [part[level] for level in range(3) for part in parts] + [one, one, one, *own]
        rows = rows + [jnp.zeros_like(one)] + [*x, one] * 2
        high, middle, low = split3(feat_ref[half, :, span].astype(F32) * gain)
        wide = jnp.concatenate(
            [high, pick_rows(rows, 24), jnp.zeros((40, TILE), F32), middle, low], axis=0
        )
        at = pl.multiple_of(offset_ref[tile] - base, 16)
        tgt_ref[pl.ds(at, TILE), :] = wide.T.astype(BF16)
        return unused

    lax.fori_loop(first, last, place, 0)
    end = offset_ref[last] - base
    blank = jnp.where(lax.broadcasted_iota(jnp.int32, (UNIT, DEPTH), 1) == 76, MASKED, 0.0)
    tgt_ref[pl.ds(pl.multiple_of(end, 16), UNIT), :] = blank.astype(BF16)
    units_ref[0] = (end + UNIT - 1) // UNIT
    units_ref[1] = core
    outlier_out_ref[0] = outlier_ref[0]


def widened(wide_ref, group, start):
    at = slice(start, start + 256)
    feat = wide_ref[group, 0:64, at]
    return jnp.concatenate([wide_ref[group, :, at], feat, feat], axis=0)


def kernel_pass(units_ref, tgt_ref, own_ref, other_ref, *refs):
    *kernel_refs, sum_ref, wide_ref, total_ref = refs
    groups = wide_ref.shape[0]
    wide_ref[:, 80:128, :] = jnp.zeros((groups, 48, GROUP), BF16)
    for lot, panel_ref in enumerate((own_ref, other_ref)):
        for piece in range(panel_ref.shape[0]):
            group, start = divmod((lot * panel_ref.shape[0] + piece) * LANES, GROUP)
            wide_ref[group, 0:80, start : start + LANES] = panel_ref[piece]

    def block(unit, count, kernel_ref=None, row=0):
        height = count * UNIT
        total_ref[0:height, :] = jnp.zeros((height, LANES), F32)

        def columns(group, unused):
            tgt = tgt_ref[unit_rows(unit, count), :]
            total = jnp.zeros((height, LANES), F32)
            for start in range(0, GROUP, 256):
                score = jnp.dot(tgt, widened(wide_ref, group, start), preferred_element_type=F32)
                rounded = jnp.exp2(score).astype(BF16)
                if kernel_ref is not None:
                    kernel_ref[group, row : row + height, start : start + 256] = rounded
                if kernel_ref is None:
                    value = rounded.astype(F32)
                    total += value[:, 0:128] + value[:, 128:256]
            if kernel_ref is not None:
                for part in range(0, height, 16):
                    lines = kernel_ref[group, row + part : row + part + 16, :].astype(F32)
                    line = lines[:, 0:128]
                    for start in range(128, GROUP, 128):
                        line += lines[:, start : start + 128]
                    total_ref[part : part + 16, :] += line
            else:
                total_ref[0:height, :] += total
            return unused

        lax.fori_loop(0, groups, columns, 0)
        for part in range(count):
            lines = total_ref[part * UNIT : (part + 1) * UNIT, :]
            sum_ref[pl.ds(unit + part, 1), :] = jnp.sum(lines.T, axis=0, keepdims=True)

    each_unit(units_ref[0], kernel_refs, block)


def unit_rows(unit, count):
    start = unit * UNIT
    return pl.ds(start if isinstance(unit, int) else pl.multiple_of(start, UNIT), count * UNIT)


def each_unit(units, kernel_refs, block):
    for index, kernel_ref in enumerate(kernel_refs):
        first = sum(KEPT[:index])
        if KEPT[index] == 2:
            pl.when(units >= first + 2)(functools.partial(block, first, 2, kernel_ref))
        pl.when(units == first + 1)(functools.partial(block, first, 1, kernel_ref))
    if KEPT[-1] == 1:
        pl.when(units > sum(KEPT))(functools.partial(block, sum(KEPT) - 1, 1, kernel_refs[-1]))

    def beyond(unit, unused):
        block(unit, 1)
        return unused

    lax.fori_loop(sum(KEPT), units, beyond, 0)


def warp_sums(acc_ref, wide_ref, anchors_ref, core, out_ref, gram_ref):
    pieces = out_ref.shape[1] // 8
    groups = wide_ref.shape[0]
    count = anchors_ref.shape[1]
    rate = 0.5 / ANCHOR_WIDTH * LOG2E
    a0, a1, a2 = anchors_ref[0:1, :], anchors_ref[1:2, :], anchors_ref[2:3, :]
    square = -(a0 * a0 + a1 * a1 + a2 * a2) * rate
    parts = [split3(row * (2.0 * rate)) for row in (a0, a1, a2)]
    zero = jnp.zeros((1, count), F32)
    rows = [part[level] for level in range(3) for part in parts] + [zero] * 3 + [*split3(square)]
    anchor_side = pick_rows(rows, LANES).T.astype(BF16)[:, 0:16]
    sums = acc_ref[...]
    sums = sums + pltpu.roll(sums, 4, 0)
    acc_ref[...] = sums
    gram_ref[...] = jnp.zeros_like(gram_ref)
    width = GROUP // 2

    def chunk(index, unused):
        at = pl.ds(pl.multiple_of(index * width, width), width)
        half = pl.ds(pl.multiple_of(index % 2 * width, width), width)
        side = wide_ref[index // 2, 64:80, half]
        y = side.astype(F32)[0:8]
        y0, y1, y2 = y[0:1], y[1:2], y[2:3]
        square = (y0 * y0 + y1 * y1 + y2 * y2) * rate
        basis = jnp.exp2(jnp.dot(anchor_side, side, preferred_element_type=F32) - square)
        moment = acc_ref[:, at]
        mass = moment[3:4, :]
        pull = moment - mass * y
        root = jnp.sqrt(mass)
        pull = pull * lax.rsqrt(jnp.maximum(mass, 1e-36))
        scaled = basis * root
        scaled_high, scaled_low = halves(scaled)
        pull_high, pull_low = halves(jnp.concatenate([pull, jnp.zeros_like(pull)], axis=0))
        last = (((1,), (1,)), ((), ()))
        left = jnp.concatenate([scaled_high, pull_high, pull_low], axis=0)
        first = lax.dot_general(left, scaled_high, last, preferred_element_type=F32)
        second = lax.dot_general(left[0:272], scaled_low, last, preferred_element_type=F32)
        gram_ref[0:288, :] += first
        gram_ref[288:560, :] += second
        return unused

    def pair(index, unused):
        chunk(index * 2, unused)
        chunk(index * 2 + 1, unused)
        return unused

    lax.fori_loop(0, groups, pair, 0)
    cross = gram_ref[288:544, :]
    gram_ref[0:256, :] += cross + cross.T
    total = jnp.sum(acc_ref[3:4, :])
    row = lax.broadcasted_iota(jnp.int32, (8, LANES), 0)
    for half in range(2):
        at = jnp.where(core == half, 0, 1)
        for r in range(GRAM_ROWS):
            out_ref[at, pl.ds(r, pieces, stride=8), :] = gram_ref[gram_place(half, r, pieces)]
        out_ref[at, pl.ds(GRAM_ROWS, pieces, stride=8), :] = jnp.zeros((pieces, LANES), F32)
        lanes = slice(half * LANES, (half + 1) * LANES)
        pulled = gram_ref[256:264, lanes] + gram_ref[272:280, lanes] + gram_ref[544:552, lanes]
        pulled = jnp.where(row == 3, total, pulled)
        for r in range(4):
            out_ref[at, r * 8 + GRAM_ROWS : r * 8 + GRAM_ROWS + 1, :] = pulled[r : r + 1]
        for piece in range(pieces):
            s = (half * pieces + piece) * LANES
            out_ref[half, piece * 8 + 7 : piece * 8 + 8, :] = acc_ref[3:4, s : s + LANES]


def gram_place(half, r, pieces):
    if half == 0:
        first, right = (r * pieces, 0) if r < 4 else ((r - 4) * pieces, 1)
    else:
        first, right = 64 + r * pieces, 1
    return slice(first, first + pieces), slice(right * LANES, (right + 1) * LANES)


def moment_pass(
    units_ref, outlier_ref, sum0_ref, sum1_ref, sum2_ref, sum3_ref, tgt_ref, wide_ref, anchors_hbm,
    *refs, total_sources,
):
    *kernel_refs, out_ref, acc_ref, gram_ref, part_ref, anchors_ref, arrived = refs
    copy = pltpu.make_async_copy(anchors_hbm, anchors_ref, arrived)
    copy.start()
    groups = wide_ref.shape[0]
    outlier = jnp.full((1, UNIT), outlier_ref[0], F32)
    floor = outlier / (1.0 - outlier) * total_sources
    acc_ref[...] = jnp.zeros_like(acc_ref)

    def block(unit, count, kernel_ref=None):
        normals = []
        for part in range(count):
            normal = floor
            for ref in (sum0_ref, sum1_ref, sum2_ref, sum3_ref):
                normal = normal + ref[pl.ds(unit + part, 1), :]
            normals.append(normal)
        side = tgt_ref[unit_rows(unit, count), 0:128].astype(F32).T[80:88]
        weight = side / jnp.concatenate(normals, axis=1)
        high = weight.astype(BF16).astype(F32)
        row = lax.broadcasted_iota(jnp.int32, weight.shape, 0)
        weight = jnp.where(row < 4, high, weight - high).astype(BF16)
        for group in range(groups):
            if kernel_ref is None:
                for start in range(0, GROUP, 256):
                    tgt = tgt_ref[unit_rows(unit, count), :]
                    score = jnp.dot(tgt, widened(wide_ref, group, start), preferred_element_type=F32)
                    part_ref[:, start : start + 256] = jnp.exp2(score).astype(BF16)
            for start in range(0, GROUP, 1024):
                at = slice(group * GROUP + start, group * GROUP + start + 1024)
                if kernel_ref is None:
                    value = part_ref[:, start : start + 1024]
                else:
                    value = kernel_ref[group, 0 : count * UNIT, start : start + 1024]
                acc_ref[:, at] += jnp.dot(weight, value, preferred_element_type=F32)

    each_unit(units_ref[0], kernel_refs, block)
    copy.wait()
    warp_sums(acc_ref, wide_ref, anchors_ref, units_ref[1], out_ref, gram_ref)


def squared_gap(first, second):
    gap_a, gap_b, gap_c = (first[c] - second[c] for c in range(3))
    return gap_a * gap_a + gap_b * gap_b + gap_c * gap_c


def halves(value):
    high = value.astype(BF16)
    return high, (value - high.astype(F32)).astype(BF16)


def dot3(first, second):
    (a, b), (c, d) = first, second
    wide = functools.partial(jnp.dot, preferred_element_type=F32)
    return wide(a, c) + (wide(a, d) + wide(b, c))


def dot_full(first, second):
    return jnp.dot(first, second, precision=lax.Precision.HIGHEST, preferred_element_type=F32)


def warp_update(
    sigma2_ref, lambda_ref, anchors_ref, xyz_ref, mass_ref, sums_ref, out_ref, out_mass_ref,
    system_ref, inverse_ref,
):
    pieces = sums_ref.shape[1] // 8
    count = anchors_ref.shape[1]
    for half in range(2):
        for r in range(GRAM_ROWS):
            system_ref[gram_place(half, r, pieces)] = sums_ref[half, pl.ds(r, pieces, stride=8), :]
    system_ref[128:256, 0:128] = system_ref[0:128, 128:256].T
    pulled = [
        jnp.concatenate([sums_ref[half, r * 8 + GRAM_ROWS : r * 8 + GRAM_ROWS + 1, :] for half in range(2)], axis=1)
        for r in range(3)
    ]
    total = sums_ref[0, 24 + GRAM_ROWS : 25 + GRAM_ROWS, 0:1]
    pulled = pick_rows(pulled, 8) / total

    rows = [anchors_ref[c : c + 1, :] for c in range(3)]
    columns = jnp.concatenate([pick_rows(rows, 8), jnp.zeros((120, count), F32)], axis=0).T
    columns = [columns[:, c : c + 1] for c in range(3)]
    rate = 0.5 / ANCHOR_WIDTH
    anchor_gram = jnp.exp(-squared_gap(columns, rows) * rate)
    place = lax.broadcasted_iota(jnp.int32, (count, count), 0)
    eye = jnp.where(place == lax.broadcasted_iota(jnp.int32, (count, count), 1), 1.0, 0.0)
    weight = lambda_ref[0] * sigma2_ref[0]
    system = system_ref[...] / total + weight * (anchor_gram + eye)
    system_ref[...] = system

    low = weight
    high = jnp.max(jnp.sum(jnp.abs(system), axis=0, keepdims=True)) * 1.0001
    start = 2.0 / jnp.full((1, count), low + high, F32)
    bound = jnp.max(jnp.full((8, LANES), high - low, F32) / jnp.full((8, LANES), high + low, F32))

    def narrowed(bound):
        square = jnp.full((8, LANES), bound * bound, F32)
        return jnp.max(2.0 / (2.0 - square)), jnp.max(square / (2.0 - square))

    scale, bound = narrowed(bound)
    inverse_ref[...] = (scale * start) * (2.0 * eye - start * system)
    system_halves = halves(system)

    def improve(bound):
        scale, after = narrowed(bound)
        inverse = inverse_ref[...]
        parts = halves(inverse)
        residual = 2.0 * eye - dot3(system_halves, parts)
        inverse_ref[...] = scale * dot3(parts, halves(residual))
        return after

    lax.while_loop(lambda bound: bound > 1e-2, improve, bound)
    inverse = inverse_ref[...]
    coeffs = dot_full(pulled, inverse)
    for _ in range(3):
        coeffs = coeffs + dot_full(pulled - dot_full(coeffs, system), inverse)

    xyz = xyz_ref[...].astype(F32)
    basis = jnp.exp(-squared_gap(columns, [xyz[c : c + 1] for c in range(3)]) * rate)
    out_ref[...] = xyz + dot_full(coeffs, basis)[0:3]
    out_mass_ref[...] = mass_ref[7:8, :]


def spread(value, axes):
    lots = jnp.broadcast_to(value, (lax.axis_size(axes), *value.shape[1:]))
    return lax.all_to_all(lots, axes, 0, 0, tiled=True)


def turned(value, axis, by):
    size = lax.axis_size(axis)
    return lax.ppermute(value, axis, [(i, (i + by) % size) for i in range(size)])


def local(
    tgt_coords, tgt_embed, tile_perm, tile_count, src_coords, src_embed, anchors, sigma2,
    outlier_weight, warp_lambda,
):
    cells = tgt_coords.shape[1]
    zs, ys, cs, xs = (lax.axis_size(name) for name in ("z", "y", "c", "x"))
    pieces = zs * ys
    sources = pieces * cs * LANES
    groups = sources // GROUP

    core = lax.axis_index("c").astype(jnp.int32)[None]
    mine = (tile_perm, tgt_coords, tgt_embed)
    inputs = (src_coords, src_embed, tile_count, *mine)
    inputs = [pltpu.with_memory_space_constraint(value, pltpu.HBM) for value in inputs]
    inputs = inputs + [turned(value, "c", 1) for value in mine]
    lots, targets, units, outlier = pl.pallas_call(
        prepare,
        in_specs=[SCALAR] * 3 + [pl.BlockSpec(memory_space=pl.ANY)] * len(inputs),
        out_specs=[WHOLE, WHOLE, SCALAR, SCALAR],
        out_shape=[
            jax.ShapeDtypeStruct((pieces, 80, LANES), BF16),
            jax.ShapeDtypeStruct((cells + TILE, DEPTH), BF16),
            jax.ShapeDtypeStruct((2,), jnp.int32),
            jax.ShapeDtypeStruct((1,), F32),
        ],
        scratch_shapes=[
            pltpu.VMEM(src_coords.shape, BF16),
            pltpu.VMEM(src_embed.shape, BF16),
            pltpu.SMEM(tile_count.shape, jnp.int32),
            pltpu.SMEM((cs, *tile_perm.shape), jnp.int32),
            pltpu.VMEM((cs, *tgt_coords.shape), BF16),
            pltpu.VMEM((cs, *tgt_embed.shape), BF16),
            pltpu.SMEM((cs * tile_perm.shape[0] + 1,), jnp.int32),
            pltpu.SemaphoreType.DMA((len(inputs),)),
        ],
        compiler_params=pltpu.CompilerParams(vmem_limit_bytes=8 << 20),
        name="prepare",
    )(core, outlier_weight, sigma2, *inputs)

    own = lax.all_to_all(lots, ("z", "y"), 0, 0, tiled=True)
    other = lax.ppermute(own, "c", [(0, 1), (1, 0)])

    *kernels, sums, wide = pl.pallas_call(
        kernel_pass,
        in_specs=[SCALAR, WHOLE, WHOLE, WHOLE],
        out_specs=[WHOLE] * (len(KEPT) + 2),
        out_shape=[
            *[jax.ShapeDtypeStruct((groups, count * UNIT, GROUP), BF16) for count in KEPT],
            jax.ShapeDtypeStruct((cells // UNIT, UNIT), F32),
            jax.ShapeDtypeStruct((groups, DEPTH // 2, GROUP), BF16),
        ],
        scratch_shapes=[pltpu.VMEM((2 * UNIT, LANES), F32)],
        compiler_params=pltpu.CompilerParams(vmem_limit_bytes=2 << 20),
        name="kernel_pass",
    )(units, targets, own, other)

    all_sums = [sums] + [turned(sums, "x", by) for by in range(1, xs)]

    share = pl.pallas_call(
        functools.partial(moment_pass, total_sources=sources * xs),
        in_specs=[SCALAR, SCALAR, *[WHOLE] * (xs + 2), pl.BlockSpec(memory_space=pltpu.HBM), *[WHOLE] * len(KEPT)],
        out_specs=WHOLE,
        out_shape=jax.ShapeDtypeStruct((cs, pieces * 8, LANES), F32),
        scratch_shapes=[
            pltpu.VMEM((8, sources), F32),
            pltpu.VMEM((560, 256), F32),
            pltpu.VMEM((UNIT, GROUP), BF16),
            pltpu.VMEM((3, 256), F32),
            pltpu.SemaphoreType.DMA,
        ],
        compiler_params=pltpu.CompilerParams(vmem_limit_bytes=5 << 20),
        name="moment_pass",
    )(units, outlier, *all_sums, targets, wide, pltpu.with_memory_space_constraint(anchors, pltpu.HBM), *kernels)

    part = share[0] + lax.ppermute(share[1], "c", [(0, 1), (1, 0)])
    part = part.reshape(pieces, 8, LANES)
    part = jnp.sum(lax.all_to_all(part, ("z", "y"), 0, 0, tiled=True), axis=0)
    total = part + turned(part, "x", 1) + turned(part, "x", 2) + turned(part, "x", 3)
    both = lax.all_gather(spread(total[None], ("z", "y")).reshape(pieces * 8, LANES), "c")

    warped, masses = pl.pallas_call(
        warp_update,
        in_specs=[SCALAR, SCALAR, WHOLE, WHOLE, WHOLE, WHOLE],
        out_specs=[WHOLE, WHOLE],
        out_shape=[jax.ShapeDtypeStruct((3, LANES), F32), jax.ShapeDtypeStruct((1, LANES), F32)],
        scratch_shapes=[pltpu.VMEM((256, 256), F32)] * 2,
        compiler_params=pltpu.CompilerParams(vmem_limit_bytes=6 << 20),
        name="warp_update",
    )(sigma2, warp_lambda, anchors, src_coords, part, both)
    return (warped, masses.reshape(LANES))


def solution(mesh):
    fine = Mesh(mesh.devices.reshape(8, 4, 2, 4), ("z", "y", "c", "x"))
    tgt = ("z", "y", "c")
    both = ("z", "y", "c", "x")
    placed = (
        P(None, tgt), P(None, tgt), P(tgt), P(), P(None, both), P(None, both), P(), P(), P(), P(),
    )
    return jax.shard_map(
        local, mesh=fine, in_specs=placed, out_specs=(P(None, both), P(both)), check_vma=False
    )
```

```python
import functools
import math

import jax
import jax.numpy as jnp
from jax import lax
from jax.experimental import pallas as pl
from jax.experimental.pallas import tpu as pltpu
from jax.sharding import Mesh
from jax.sharding import PartitionSpec as P

TILE = 512
SCORE_GAIN = 4.0
ANCHOR_WIDTH = 0.1
LOG2E = math.log2(math.e)

UNIT = 256
LANES = 128
GROUP = 2048
DEPTH = 256
KEPT = (2, 2, 2, 2, 2, 1)
MASKED = -30000.0
GRAM_ROWS = 6

F32 = jnp.float32
BF16 = jnp.bfloat16
WHOLE = pl.BlockSpec(memory_space=pltpu.VMEM)
SCALAR = pl.BlockSpec(memory_space=pltpu.SMEM)


def split3(value):
    high = value.astype(BF16).astype(F32)
    rest = value - high
    middle = rest.astype(BF16).astype(F32)
    return high, middle, rest - middle


def pick_rows(rows, count):
    width = rows[0].shape[1]
    place = lax.broadcasted_iota(jnp.int32, (count, width), 0)
    out = jnp.zeros((count, width), F32)
    for index, row in enumerate(rows):
        out = jnp.where(place == index, row, out)
    return out


def prepare(
    core_ref, outlier_ref, sigma2_ref, src_xyz_hbm, src_feat_hbm, count_hbm, perm_hbm, xyz_hbm, feat_hbm,
    other_perm_hbm, other_xyz_hbm, other_feat_hbm, lots_ref, tgt_ref, units_ref, outlier_out_ref,
    src_xyz_ref, src_feat_ref, count_ref, perm_ref, xyz_ref, feat_ref, offset_ref, arrived,
):
    core = core_ref[0]
    pairs = [
        (src_xyz_hbm, src_xyz_ref), (src_feat_hbm, src_feat_ref), (count_hbm, count_ref),
        (perm_hbm, perm_ref.at[core]), (other_perm_hbm, perm_ref.at[1 - core]),
        (xyz_hbm, xyz_ref.at[core]), (other_xyz_hbm, xyz_ref.at[1 - core]),
        (feat_hbm, feat_ref.at[core]), (other_feat_hbm, feat_ref.at[1 - core]),
    ]
    copies = [pltpu.make_async_copy(*pair, arrived.at[index]) for index, pair in enumerate(pairs)]
    for copy in copies:
        copy.start()
    for copy in copies[:2]:
        copy.wait()
    one = jnp.ones((1, LANES), F32)
    inv = (0.5 * LOG2E) / jnp.full((1, LANES), sigma2_ref[0], F32)
    y = src_xyz_ref[...].astype(F32)
    y = [y[c : c + 1] for c in range(3)]
    square = -(y[0] * y[0] + y[1] * y[1] + y[2] * y[2]) * inv
    side = pick_rows([*y, *y, *y, *split3(square), one, one, one], 16)
    source = jnp.concatenate([src_feat_ref[...], side.astype(BF16)], axis=0)
    for lot in range(lots_ref.shape[0]):
        lots_ref[lot] = source

    for copy in copies[2:]:
        copy.wait()
    gain = SCORE_GAIN / 64 * LOG2E
    inv = (0.5 * LOG2E) / jnp.full((1, TILE), sigma2_ref[0], F32)
    one = jnp.ones((1, TILE), F32)
    lane = lax.broadcasted_iota(jnp.int32, (1, TILE), 1)

    tiles = perm_ref.shape[1]
    offset = jnp.int32(0)
    for tile in range(2 * tiles):
        offset_ref[tile] = offset
        count = count_ref[perm_ref[tile // tiles, tile % tiles]]
        offset = offset + ((count + 15) // 16) * 16
    offset_ref[2 * tiles] = offset
    split = jnp.int32(tiles)
    least = jnp.maximum(offset_ref[tiles], offset - offset_ref[tiles])
    for tile in range(1, 2 * tiles):
        most = jnp.maximum(offset_ref[tile], offset - offset_ref[tile])
        split = jnp.where(most < least, tile, split)
        least = jnp.minimum(most, least)
    first = jnp.where(core == 0, 0, split)
    last = jnp.where(core == 0, split, 2 * tiles)
    base = offset_ref[first]

    def place(tile, unused):
        half = (tile >= tiles).astype(jnp.int32)
        slot = tile - half * tiles
        span = pl.ds(pl.multiple_of(slot * TILE, TILE), TILE)
        count = count_ref[perm_ref[half, slot]]
        xyz = xyz_ref[half, :, span].astype(F32)
        x = [xyz[c : c + 1] for c in range(3)]
        square = -(x[0] * x[0] + x[1] * x[1] + x[2] * x[2]) * inv
        parts = [split3(row * (2.0 * inv)) for row in x]
        own = split3(jnp.where(lane < count, square, MASKED))
        rows = [part[level] for level in range(3) for part in parts] + [one, one, one, *own]
        rows = rows + [jnp.zeros_like(one)] + [*x, one] * 2
        high, middle, low = split3(feat_ref[half, :, span].astype(F32) * gain)
        wide = jnp.concatenate(
            [high, pick_rows(rows, 24), jnp.zeros((40, TILE), F32), middle, low], axis=0
        )
        at = pl.multiple_of(offset_ref[tile] - base, 16)
        tgt_ref[pl.ds(at, TILE), :] = wide.astype(BF16).T
        return unused

    lax.fori_loop(first, last, place, 0)
    end = offset_ref[last] - base
    blank = jnp.where(lax.broadcasted_iota(jnp.int32, (UNIT, DEPTH), 1) == 76, MASKED, 0.0)
    tgt_ref[pl.ds(pl.multiple_of(end, 16), UNIT), :] = blank.astype(BF16)
    units_ref[0] = (end + UNIT - 1) // UNIT
    units_ref[1] = core
    outlier_out_ref[0] = outlier_ref[0]


def widened(wide_ref, group, start):
    at = slice(start, start + 256)
    feat = wide_ref[group, 0:64, at]
    return jnp.concatenate([wide_ref[group, :, at], feat, feat], axis=0)


def kernel_pass(units_ref, tgt_ref, own_ref, other_ref, *refs):
    *kernel_refs, sum_ref, wide_ref, total_ref = refs
    groups = wide_ref.shape[0]
    wide_ref[:, 80:128, :] = jnp.zeros((groups, 48, GROUP), BF16)
    for lot, panel_ref in enumerate((own_ref, other_ref)):
        for piece in range(panel_ref.shape[0]):
            group, start = divmod((lot * panel_ref.shape[0] + piece) * LANES, GROUP)
            wide_ref[group, 0:80, start : start + LANES] = panel_ref[piece]

    def block(unit, count, kernel_ref=None, row=0):
        height = count * UNIT
        total_ref[0:height, :] = jnp.zeros((height, LANES), F32)

        def columns(group, unused):
            tgt = tgt_ref[unit_rows(unit, count), :]
            total = jnp.zeros((height, LANES), F32)
            for start in range(0, GROUP, 256):
                score = jnp.dot(tgt, widened(wide_ref, group, start), preferred_element_type=F32)
                rounded = jnp.exp2(score).astype(BF16)
                if kernel_ref is not None:
                    kernel_ref[group, row : row + height, start : start + 256] = rounded
                if kernel_ref is None:
                    value = rounded.astype(F32)
                    total += value[:, 0:128] + value[:, 128:256]
            if kernel_ref is not None:
                for part in range(0, height, 16):
                    lines = kernel_ref[group, row + part : row + part + 16, :].astype(F32)
                    line = lines[:, 0:128]
                    for start in range(128, GROUP, 128):
                        line += lines[:, start : start + 128]
                    total_ref[part : part + 16, :] += line
            else:
                total_ref[0:height, :] += total
            return unused

        lax.fori_loop(0, groups, columns, 0)
        for part in range(count):
            lines = total_ref[part * UNIT : (part + 1) * UNIT, :]
            sum_ref[pl.ds(unit + part, 1), :] = jnp.sum(lines.T, axis=0, keepdims=True)

    each_unit(units_ref[0], kernel_refs, block)


def unit_rows(unit, count):
    start = unit * UNIT
    return pl.ds(start if isinstance(unit, int) else pl.multiple_of(start, UNIT), count * UNIT)


def each_unit(units, kernel_refs, block):
    for index, kernel_ref in enumerate(kernel_refs):
        first = sum(KEPT[:index])
        if KEPT[index] == 2:
            pl.when(units >= first + 2)(functools.partial(block, first, 2, kernel_ref))
        pl.when(units == first + 1)(functools.partial(block, first, 1, kernel_ref))
    if KEPT[-1] == 1:
        pl.when(units > sum(KEPT))(functools.partial(block, sum(KEPT) - 1, 1, kernel_refs[-1]))

    def beyond(unit, unused):
        block(unit, 1)
        return unused

    lax.fori_loop(sum(KEPT), units, beyond, 0)


def warp_sums(acc_ref, wide_ref, anchors_ref, core, out_ref, gram_ref):
    pieces = out_ref.shape[1] // 8
    groups = wide_ref.shape[0]
    count = anchors_ref.shape[1]
    rate = 0.5 / ANCHOR_WIDTH * LOG2E
    a0, a1, a2 = anchors_ref[0:1, :], anchors_ref[1:2, :], anchors_ref[2:3, :]
    square = -(a0 * a0 + a1 * a1 + a2 * a2) * rate
    parts = [split3(row * (2.0 * rate)) for row in (a0, a1, a2)]
    zero = jnp.zeros((1, count), F32)
    rows = [part[level] for level in range(3) for part in parts] + [zero] * 3 + [*split3(square)]
    anchor_side = pick_rows(rows, LANES).T.astype(BF16)[:, 0:16]
    sums = acc_ref[...]
    sums = sums + pltpu.roll(sums, 4, 0)
    acc_ref[...] = sums
    gram_ref[...] = jnp.zeros_like(gram_ref)
    width = GROUP // 2

    def chunk(index, unused):
        at = pl.ds(pl.multiple_of(index * width, width), width)
        half = pl.ds(pl.multiple_of(index % 2 * width, width), width)
        side = wide_ref[index // 2, 64:80, half]
        y = side.astype(F32)[0:8]
        y0, y1, y2 = y[0:1], y[1:2], y[2:3]
        square = (y0 * y0 + y1 * y1 + y2 * y2) * rate
        basis = jnp.exp2(jnp.dot(anchor_side, side, preferred_element_type=F32) - square)
        moment = acc_ref[:, at]
        mass = moment[3:4, :]
        pull = moment - mass * y
        root = jnp.sqrt(mass)
        pull = pull * lax.rsqrt(jnp.maximum(mass, 1e-36))
        scaled = basis * root
        scaled_high, scaled_low = halves(scaled)
        pull_high, pull_low = halves(jnp.concatenate([pull, jnp.zeros_like(pull)], axis=0))
        last = (((1,), (1,)), ((), ()))
        left = jnp.concatenate([scaled_high, pull_high, pull_low], axis=0)
        first = lax.dot_general(left, scaled_high, last, preferred_element_type=F32)
        second = lax.dot_general(left[0:272], scaled_low, last, preferred_element_type=F32)
        gram_ref[0:288, :] += first
        gram_ref[288:560, :] += second
        return unused

    def pair(index, unused):
        chunk(index * 2, unused)
        chunk(index * 2 + 1, unused)
        return unused

    lax.fori_loop(0, groups, pair, 0)
    cross = gram_ref[288:544, :]
    gram_ref[0:256, :] += cross + cross.T
    total = jnp.sum(acc_ref[3:4, :])
    row = lax.broadcasted_iota(jnp.int32, (8, LANES), 0)
    for half in range(2):
        at = jnp.where(core == half, 0, 1)
        for r in range(GRAM_ROWS):
            out_ref[at, pl.ds(r, pieces, stride=8), :] = gram_ref[gram_place(half, r, pieces)]
        out_ref[at, pl.ds(GRAM_ROWS, pieces, stride=8), :] = jnp.zeros((pieces, LANES), F32)
        lanes = slice(half * LANES, (half + 1) * LANES)
        pulled = gram_ref[256:264, lanes] + gram_ref[272:280, lanes] + gram_ref[544:552, lanes]
        pulled = jnp.where(row == 3, total, pulled)
        for r in range(4):
            out_ref[at, r * 8 + GRAM_ROWS : r * 8 + GRAM_ROWS + 1, :] = pulled[r : r + 1]
        for piece in range(pieces):
            s = (half * pieces + piece) * LANES
            out_ref[half, piece * 8 + 7 : piece * 8 + 8, :] = acc_ref[3:4, s : s + LANES]


def gram_place(half, r, pieces):
    if half == 0:
        first, right = (r * pieces, 0) if r < 4 else ((r - 4) * pieces, 1)
    else:
        first, right = 64 + r * pieces, 1
    return slice(first, first + pieces), slice(right * LANES, (right + 1) * LANES)


def moment_pass(
    units_ref, outlier_ref, sum0_ref, sum1_ref, sum2_ref, sum3_ref, tgt_ref, wide_ref, anchors_hbm,
    *refs, total_sources,
):
    *kernel_refs, out_ref, acc_ref, gram_ref, part_ref, anchors_ref, arrived = refs
    copy = pltpu.make_async_copy(anchors_hbm, anchors_ref, arrived)
    copy.start()
    groups = wide_ref.shape[0]
    outlier = jnp.full((1, UNIT), outlier_ref[0], F32)
    floor = outlier / (1.0 - outlier) * total_sources
    acc_ref[...] = jnp.zeros_like(acc_ref)

    def block(unit, count, kernel_ref=None):
        normals = []
        for part in range(count):
            normal = floor
            for ref in (sum0_ref, sum1_ref, sum2_ref, sum3_ref):
                normal = normal + ref[pl.ds(unit + part, 1), :]
            normals.append(normal)
        side = tgt_ref[unit_rows(unit, count), 0:128].astype(F32).T[80:88]
        weight = side / jnp.concatenate(normals, axis=1)
        high = weight.astype(BF16).astype(F32)
        row = lax.broadcasted_iota(jnp.int32, weight.shape, 0)
        weight = jnp.where(row < 4, high, weight - high).astype(BF16)
        for group in range(groups):
            if kernel_ref is None:
                for start in range(0, GROUP, 256):
                    tgt = tgt_ref[unit_rows(unit, count), :]
                    score = jnp.dot(tgt, widened(wide_ref, group, start), preferred_element_type=F32)
                    part_ref[:, start : start + 256] = jnp.exp2(score).astype(BF16)
            for start in range(0, GROUP, 1024):
                at = slice(group * GROUP + start, group * GROUP + start + 1024)
                if kernel_ref is None:
                    value = part_ref[:, start : start + 1024]
                else:
                    value = kernel_ref[group, 0 : count * UNIT, start : start + 1024]
                acc_ref[:, at] += jnp.dot(weight, value, preferred_element_type=F32)

    each_unit(units_ref[0], kernel_refs, block)
    copy.wait()
    warp_sums(acc_ref, wide_ref, anchors_ref, units_ref[1], out_ref, gram_ref)


def squared_gap(first, second):
    gap_a, gap_b, gap_c = (first[c] - second[c] for c in range(3))
    return gap_a * gap_a + gap_b * gap_b + gap_c * gap_c


def halves(value):
    high = value.astype(BF16)
    return high, (value - high.astype(F32)).astype(BF16)


def dot3(first, second):
    (a, b), (c, d) = first, second
    wide = functools.partial(jnp.dot, preferred_element_type=F32)
    return wide(a, c) + (wide(a, d) + wide(b, c))


def dot_full(first, second):
    return jnp.dot(first, second, precision=lax.Precision.HIGHEST, preferred_element_type=F32)


def warp_update(
    units_ref, sigma2_ref, lambda_ref, anchors_ref, xyz_ref, mass_ref, own_ref, other_ref, out_ref, out_mass_ref,
    system_ref, inverse_ref, sums_ref,
):
    core = units_ref[1]
    sums_ref[core] = own_ref[...]
    sums_ref[1 - core] = other_ref[...]
    pieces = sums_ref.shape[1] // 8
    count = anchors_ref.shape[1]
    for half in range(2):
        for r in range(GRAM_ROWS):
            system_ref[gram_place(half, r, pieces)] = sums_ref[half, pl.ds(r, pieces, stride=8), :]
    system_ref[128:256, 0:128] = system_ref[0:128, 128:256].T
    pulled = [
        jnp.concatenate([sums_ref[half, r * 8 + GRAM_ROWS : r * 8 + GRAM_ROWS + 1, :] for half in range(2)], axis=1)
        for r in range(3)
    ]
    total = sums_ref[0, 24 + GRAM_ROWS : 25 + GRAM_ROWS, 0:1]
    pulled = pick_rows(pulled, 8) / total

    rows = [anchors_ref[c : c + 1, :] for c in range(3)]
    columns = jnp.concatenate([pick_rows(rows, 8), jnp.zeros((120, count), F32)], axis=0).T
    columns = [columns[:, c : c + 1] for c in range(3)]
    rate = 0.5 / ANCHOR_WIDTH
    anchor_gram = jnp.exp(-squared_gap(columns, rows) * rate)
    place = lax.broadcasted_iota(jnp.int32, (count, count), 0)
    eye = jnp.where(place == lax.broadcasted_iota(jnp.int32, (count, count), 1), 1.0, 0.0)
    weight = lambda_ref[0] * sigma2_ref[0]
    system = system_ref[...] / total + weight * (anchor_gram + eye)
    system_ref[...] = system

    low = weight
    high = jnp.max(jnp.sum(jnp.abs(system), axis=0, keepdims=True)) * 1.0001
    start = 2.0 / jnp.full((1, count), low + high, F32)
    bound = jnp.max(jnp.full((8, LANES), high - low, F32) / jnp.full((8, LANES), high + low, F32))

    def narrowed(bound):
        square = jnp.full((8, LANES), bound * bound, F32)
        return jnp.max(2.0 / (2.0 - square)), jnp.max(square / (2.0 - square))

    scale, bound = narrowed(bound)
    inverse_ref[...] = (scale * start) * (2.0 * eye - start * system)
    system_halves = halves(system)

    def improve(bound):
        scale, after = narrowed(bound)
        inverse = inverse_ref[...]
        parts = halves(inverse)
        residual = 2.0 * eye - dot3(system_halves, parts)
        inverse_ref[...] = scale * dot3(parts, halves(residual))
        return after

    lax.while_loop(lambda bound: bound > 1e-2, improve, bound)
    inverse = inverse_ref[...]
    coeffs = dot_full(pulled, inverse)
    for _ in range(3):
        coeffs = coeffs + dot_full(pulled - dot_full(coeffs, system), inverse)

    xyz = xyz_ref[...].astype(F32)
    basis = jnp.exp(-squared_gap(columns, [xyz[c : c + 1] for c in range(3)]) * rate)
    out_ref[...] = xyz + dot_full(coeffs, basis)[0:3]
    out_mass_ref[...] = mass_ref[7:8, :]


def spread(value, axes):
    lots = jnp.broadcast_to(value, (lax.axis_size(axes), *value.shape[1:]))
    return lax.all_to_all(lots, axes, 0, 0, tiled=True)


def turned(value, axis, by):
    size = lax.axis_size(axis)
    return lax.ppermute(value, axis, [(i, (i + by) % size) for i in range(size)])


def local(
    tgt_coords, tgt_embed, tile_perm, tile_count, src_coords, src_embed, anchors, sigma2,
    outlier_weight, warp_lambda,
):
    cells = tgt_coords.shape[1]
    zs, ys, cs, xs = (lax.axis_size(name) for name in ("z", "y", "c", "x"))
    pieces = zs * ys
    sources = pieces * cs * LANES
    groups = sources // GROUP

    core = lax.axis_index("c").astype(jnp.int32)[None]
    mine = (tile_perm, tgt_coords, tgt_embed)
    inputs = (src_coords, src_embed, tile_count, *mine)
    inputs = [pltpu.with_memory_space_constraint(value, pltpu.HBM) for value in inputs]
    inputs = inputs + [turned(value, "c", 1) for value in mine]
    lots, targets, units, outlier = pl.pallas_call(
        prepare,
        in_specs=[SCALAR] * 3 + [pl.BlockSpec(memory_space=pl.ANY)] * len(inputs),
        out_specs=[WHOLE, WHOLE, SCALAR, SCALAR],
        out_shape=[
            jax.ShapeDtypeStruct((pieces, 80, LANES), BF16),
            jax.ShapeDtypeStruct((cells + TILE, DEPTH), BF16),
            jax.ShapeDtypeStruct((2,), jnp.int32),
            jax.ShapeDtypeStruct((1,), F32),
        ],
        scratch_shapes=[
            pltpu.VMEM(src_coords.shape, BF16),
            pltpu.VMEM(src_embed.shape, BF16),
            pltpu.SMEM(tile_count.shape, jnp.int32),
            pltpu.SMEM((cs, *tile_perm.shape), jnp.int32),
            pltpu.VMEM((cs, *tgt_coords.shape), BF16),
            pltpu.VMEM((cs, *tgt_embed.shape), BF16),
            pltpu.SMEM((cs * tile_perm.shape[0] + 1,), jnp.int32),
            pltpu.SemaphoreType.DMA((len(inputs),)),
        ],
        compiler_params=pltpu.CompilerParams(vmem_limit_bytes=8 << 20),
        name="prepare",
    )(core, outlier_weight, sigma2, *inputs)

    own = lax.all_to_all(lots, ("z", "y"), 0, 0, tiled=True)
    other = lax.ppermute(own, "c", [(0, 1), (1, 0)])

    *kernels, sums, wide = pl.pallas_call(
        kernel_pass,
        in_specs=[SCALAR, WHOLE, WHOLE, WHOLE],
        out_specs=[WHOLE] * (len(KEPT) + 2),
        out_shape=[
            *[jax.ShapeDtypeStruct((groups, count * UNIT, GROUP), BF16) for count in KEPT],
            jax.ShapeDtypeStruct((cells // UNIT, UNIT), F32),
            jax.ShapeDtypeStruct((groups, DEPTH // 2, GROUP), BF16),
        ],
        scratch_shapes=[pltpu.VMEM((2 * UNIT, LANES), F32)],
        compiler_params=pltpu.CompilerParams(vmem_limit_bytes=2 << 20),
        name="kernel_pass",
    )(units, targets, own, other)

    all_sums = [sums] + [turned(sums, "x", by) for by in range(1, xs)]

    share = pl.pallas_call(
        functools.partial(moment_pass, total_sources=sources * xs),
        in_specs=[SCALAR, SCALAR, *[WHOLE] * (xs + 2), pl.BlockSpec(memory_space=pltpu.HBM), *[WHOLE] * len(KEPT)],
        out_specs=WHOLE,
        out_shape=jax.ShapeDtypeStruct((cs, pieces * 8, LANES), F32),
        scratch_shapes=[
            pltpu.VMEM((8, sources), F32),
            pltpu.VMEM((560, 256), F32),
            pltpu.VMEM((UNIT, GROUP), BF16),
            pltpu.VMEM((3, 256), F32),
            pltpu.SemaphoreType.DMA,
        ],
        compiler_params=pltpu.CompilerParams(vmem_limit_bytes=5 << 20),
        name="moment_pass",
    )(units, outlier, *all_sums, targets, wide, pltpu.with_memory_space_constraint(anchors, pltpu.HBM), *kernels)

    part = share[0] + lax.ppermute(share[1], "c", [(0, 1), (1, 0)])
    part = part.reshape(pieces, 8, LANES)
    part = jnp.sum(lax.all_to_all(part, ("z", "y"), 0, 0, tiled=True), axis=0)
    total = part + turned(part, "x", 1) + turned(part, "x", 2) + turned(part, "x", 3)
    mine = spread(total[None], ("z", "y")).reshape(pieces * 8, LANES)
    others = turned(mine, "c", 1)

    warped, masses = pl.pallas_call(
        warp_update,
        in_specs=[SCALAR] * 3 + [WHOLE] * 5,
        out_specs=[WHOLE, WHOLE],
        out_shape=[jax.ShapeDtypeStruct((3, LANES), F32), jax.ShapeDtypeStruct((1, LANES), F32)],
        scratch_shapes=[pltpu.VMEM((256, 256), F32)] * 2 + [pltpu.VMEM((cs, pieces * 8, LANES), F32)],
        compiler_params=pltpu.CompilerParams(vmem_limit_bytes=6 << 20),
        name="warp_update",
    )(units, sigma2, warp_lambda, anchors, src_coords, part, mine, others)
    return (warped, masses.reshape(LANES))


def solution(mesh):
    fine = Mesh(mesh.devices.reshape(8, 4, 2, 4), ("z", "y", "c", "x"))
    tgt = ("z", "y", "c")
    both = ("z", "y", "c", "x")
    placed = (
        P(None, tgt), P(None, tgt), P(tgt), P(), P(None, both), P(None, both), P(), P(), P(), P(),
    )
    return jax.shard_map(
        local, mesh=fine, in_specs=placed, out_specs=(P(None, both), P(both)), check_vma=False
    )
```
